128 devices in a mesh: group: 2 (over x_hi), seq: 8 (over y, x_lo), tp: 8 (over z, core).
Axes of the slice: x: 4 (x_hi: 2, x_lo: 2; x = x_hi * 2 + x_lo), y: 4, z: 4, core: 2. Of those that a mesh axis runs over, the one named last changes fastest.
Arguments:
- prompt_tokens: bfloat16 [2, 4096, 5120], P(None, ('group', 'seq')), may hold values from -6 to 6
- prompt_lengths: int32 [2], replicated, may hold values from 1024 to 4096
- prompt_token_start: int32 [2], replicated, may hold values from 0 to 12287
- block_owner: int32 [128, 2, 1], P(('group', 'seq')), may hold values from 0 to 15; in each aligned block of 16 rows (0 to 15, 16 to 31, ..., all dimensions but the last counted through in order) at most 2 rows name the same one
- decode_hidden: bfloat16 [128, 4, 5120], P(('group', 'seq')), may hold values from -6 to 6
- cache_lengths: int32 [128], P(('group', 'seq')), may hold values from 1 to 1024
- key_cache: bfloat16 [128, 1024, 1024], P(('group', 'seq'), None, 'tp'), may hold values from -6 to 6
- value_cache: bfloat16 [128, 1024, 1024], P(('group', 'seq'), None, 'tp'), may hold values from -6 to 6
- w_query: bfloat16 [5120, 4096], P(None, 'tp'), may hold values from -0.078125 to 0.078125
- w_key: bfloat16 [5120, 1024], P(None, 'tp'), may hold values from -0.078125 to 0.078125
- w_value: bfloat16 [5120, 1024], P(None, 'tp'), may hold values from -0.078125 to 0.078125
- w_out: bfloat16 [4096, 5120], P('tp'), may hold values from -0.5 to 0.5
- query_gain: float32 [128], replicated, may hold values from 0.5 to 8
- key_gain: float32 [128], replicated, may hold values from 0.5 to 8
Outputs:
- prefill_context: bfloat16 [2, 4096, 4096], P(None, ('group', 'seq'), 'tp')
- kv_pool: bfloat16 [16, 32, 32, 2, 1024], P(('group', 'seq'), None, None, None, 'tp')
- decode_out: bfloat16 [128, 4, 5120], P(('group', 'seq'))
The draws below stay inside these ranges and needn't reach their ends.
Inputs may be any that keep to these rules, and one draw needn't show every extreme that they name: `block_owner`: in the rows of one index of group and seq (16 rows), no owner is named more than 2 times.
All inputs are finite; a program needn't handle non-finite values.
Results may differ from the reference program's by a relative error of at most 0.019.
The reference program's roundings to bfloat16 on the way (of `values`) count: a program that leaves them out, or rounds other values in their place, can miss the bound.
Values may be sent and summed in bfloat16 or wider, within the bound.
A program may use at most 192 MiB of HBM per device.

```python
import math
import jax
import jax.numpy as jnp
import numpy as np
from jax import lax

D = 5120
HD = 128
HEADS = 32
KVH = 8
SPAN = 4096
PROMPTS = 2
BLK = 32
STEPS = 4
CACHE = 1024
SHARDS = 16
CT = 256
NB_DEV = 16
CAP = 2
ROWS = 128


def draw_query_gain(key, part):
    key = jax.random.fold_in(key, 11)
    return jax.random.uniform(key, (HD,), jnp.float32, 0.5, 2.5)


def draw_key_gain(key, part):
    key = jax.random.fold_in(key, 23)
    return jax.random.uniform(key, (HD,), jnp.float32, 0.5, 2.5)


def plant(result, key, least, high):
    spot = [jax.random.randint(jax.random.fold_in(key, axis), (), 0, length) for axis, length in enumerate(result.shape)]
    main_axis = result.shape.index(max(result.shape))
    neighbour = spot[:main_axis] + [(spot[main_axis] + 1) % result.shape[main_axis]] + spot[main_axis + 1:]
    return result.at[tuple(spot)].set(least).at[tuple(neighbour)].set(high)


def levels(key, extent, pieces, low, top_value):
    level = 1.0
    for axis_at, blocks in pieces:
        heights = jax.random.uniform(jax.random.fold_in(jax.random.fold_in(key, 6), axis_at), (blocks,), jnp.float32, low / len(pieces), top_value / len(pieces))
        level = level * jnp.repeat(jnp.exp(heights), extent[axis_at] // blocks).reshape((-1,) + (1,) * (len(extent) - 1 - axis_at))
    return level


def deal_out(key, own, number, rows, amount, top, bound, skew):
    order = jax.random.permutation(key, amount)
    heavy_load, common = shares(amount, rows * top, bound, skew, True), shares(amount, rows * top, bound, skew, False)
    places = jnp.arange(amount)

    def named(tallies, rotation):
        used = int((tallies > 0).sum())
        fixed = max(1, used // 4)
        moved = fixed + (places - fixed + rotation * (used - fixed)) % max(1, amount - fixed)
        return jnp.zeros((amount,), jnp.int32).at[order[jnp.where(places < fixed, places, moved)]].set(jnp.asarray(tallies, jnp.int32))

    tallies = jnp.where(number % 4 == 0, named(heavy_load, number // 4), named(common, number - number // 4 - 1))
    mixed = jax.random.permutation(jax.random.fold_in(own, 3), amount)
    donor, taker = mixed[0:amount // 2 * 2:2], mixed[1:amount // 2 * 2:2]
    room = jnp.minimum(tallies[donor] - 1, bound - tallies[taker]) // 2
    room = jnp.where((donor == order[0]) | (taker == order[0]) | (tallies[taker] == 0), 0, jnp.maximum(room, 0))
    moved = jax.random.randint(jax.random.fold_in(own, 4), (amount // 2,), 0, 1 << 20) % (room + 1)
    tallies = tallies.at[donor].add(-moved).at[taker].add(moved)
    labels = jnp.searchsorted(jnp.cumsum(tallies), jnp.arange(rows * top), side="right").astype(jnp.int32)
    table = labels.reshape(top, rows).T
    table = table[jax.random.permutation(jax.random.fold_in(own, 1), rows)]
    rotation = jax.random.randint(jax.random.fold_in(own, 2), (rows, 1), 0, top)
    return jnp.take_along_axis(table, (jnp.arange(top)[None, :] + rotation) % top, axis=1)


def shares(amount, total, limit, slope, full):
    loads = [(1 << 20) // math.isqrt(grade ** slope) + 1 for grade in range(1, amount + 1)]
    largest = limit if full else min(limit, max(-(-total // amount), total * loads[0] // sum(loads)))
    least = 1 if total - largest >= amount - 1 else 0
    counts, rest = [largest] + [least] * (amount - 1), total - largest - least * (amount - 1)
    while rest > 0:
        free = [i for i in range(1, amount) if counts[i] < largest] or [i for i in range(1, amount) if counts[i] < limit]
        mass, budget = sum([loads[i] for i in free]), rest
        for i in free:
            more = min(limit - counts[i], max(1, budget * loads[i] // mass), rest)
            counts[i] = counts[i] + more
            rest = rest - more
    return np.array(counts)


def scatter_about(stream_key, extent, scale, most, pieces=(), held_as=jnp.bfloat16):
    factor_of = levels(stream_key, extent, pieces, -0.22, 0.18) if pieces else 1.0
    array = jax.random.normal(stream_key, extent, jnp.float32) * scale * factor_of
    return jnp.minimum(jnp.maximum(array, -most), most).astype(held_as)


def setup_inputs(seed: int = 0) -> dict:
    key_list = jax.random.split(jax.random.key(seed), 15)
    prompt_tokens = scatter_about(key_list[0], (PROMPTS, SPAN, D), 1.0, 6.0, ((1, 16),))
    prompt_lengths = jax.random.randint(key_list[1], (PROMPTS,), SPAN // 4, SPAN + 1).astype(jnp.int32)
    prompt_token_start = jax.random.randint(key_list[2], (PROMPTS,), 0, 3 * SPAN).astype(jnp.int32)
    block_owner_keys = jax.random.split(jax.random.fold_in(key_list[3], 1), (SPAN // BLK) * PROMPTS // NB_DEV)
    block_owner_turns = jax.random.permutation(jax.random.fold_in(key_list[3], 3), (SPAN // BLK) * PROMPTS // NB_DEV)
    block_owner = jax.vmap(lambda own, number: deal_out(jax.random.fold_in(key_list[3], 2), own, number, NB_DEV, SHARDS, 1, CAP, 1))(block_owner_keys, block_owner_turns).reshape((SPAN // BLK, PROMPTS, 1))
    decode_hidden = scatter_about(key_list[4], (ROWS, STEPS, D), 1.0, 6.0, ((0, 16),))
    cache_lengths = plant(jax.random.randint(key_list[5], (ROWS,), 1, CACHE + 1), jax.random.fold_in(key_list[5], 1), 1, CACHE).astype(jnp.int32)
    key_cache = scatter_about(key_list[6], (ROWS, CACHE, KVH * HD), 1.0, 6.0, ((0, 16), (2, 8)))
    value_cache = scatter_about(key_list[7], (ROWS, CACHE, KVH * HD), 1.0, 6.0, ((0, 16), (2, 8)))
    w_query = scatter_about(key_list[8], (D, HEADS * HD), D ** -0.5, 0.078125, ((1, 8),))
    w_key = scatter_about(key_list[9], (D, KVH * HD), D ** -0.5, 0.078125, ((1, 8),))
    w_value = scatter_about(key_list[10], (D, KVH * HD), D ** -0.5, 0.078125, ((1, 8),))
    w_out = scatter_about(key_list[11], (HEADS * HD, D), HD ** -0.5, 0.5, ((0, 8),))
    query_gain = draw_query_gain(jax.random.fold_in(key_list[14], 71), 0)
    key_gain = draw_key_gain(jax.random.fold_in(key_list[14], 71), 0)
    return {"prompt_tokens": prompt_tokens, "prompt_lengths": prompt_lengths, "prompt_token_start": prompt_token_start, "block_owner": block_owner, "decode_hidden": decode_hidden, "cache_lengths": cache_lengths, "key_cache": key_cache, "value_cache": value_cache, "w_query": w_query, "w_key": w_key, "w_value": w_value, "w_out": w_out, "query_gain": query_gain, "key_gain": key_gain}


eps = 1e-06
theta = 1000000.0

def head_norm(raw, gain):
    mean_sq = lax.optimization_barrier(jnp.mean(raw * raw, axis=-1, keepdims=True))
    return raw * lax.rsqrt(mean_sq + eps) * gain

def rotate(raw, positions):
    half = raw.shape[-1] // 2
    freqs = theta ** (-jnp.arange(half, dtype=jnp.float32) * 2.0 / raw.shape[-1])
    angles = positions[..., None, None] * freqs
    cosine = jnp.cos(angles)
    sine = jnp.sin(angles)
    first = raw[..., :half]
    second = raw[..., half:]
    return jnp.concatenate([first * cosine - second * sine, second * cosine + first * sine], axis=-1)

def project(hidden, weight, heads, gain, positions):
    raw = jnp.dot(hidden.reshape(-1, hidden.shape[-1]), weight, preferred_element_type=jnp.float32)
    raw = raw.reshape(hidden.shape[:-1] + (heads, -1))
    return rotate(head_norm(raw, gain), positions).astype(jnp.bfloat16)

def plain_values(hidden, weight, heads):
    raw = jnp.dot(hidden.reshape(-1, hidden.shape[-1]), weight, preferred_element_type=jnp.float32)
    return raw.astype(jnp.bfloat16).reshape(hidden.shape[:-1] + (heads, -1))

def reference(prompt_tokens, prompt_lengths, prompt_token_start, block_owner, decode_hidden, cache_lengths, key_cache, value_cache, w_query, w_key, w_value, w_out, query_gain, key_gain):
    group_size = HEADS // KVH
    scale = HD ** (-0.5)
    positions = prompt_token_start[:, None].astype(jnp.float32) + jnp.arange(SPAN, dtype=jnp.float32)[None, :]
    queries = project(prompt_tokens, w_query, HEADS, query_gain, positions)
    keys = project(prompt_tokens, w_key, KVH, key_gain, positions)
    values = plain_values(prompt_tokens, w_value, KVH)
    qrows = min(SPAN, 512)
    nqb = SPAN // qrows
    q_items = queries.reshape(PROMPTS, nqb, qrows, KVH, group_size, HD).transpose(0, 3, 1, 2, 4, 5)
    q_items = q_items.reshape(PROMPTS * KVH * nqb, qrows, group_size, HD)
    k_heads = keys.transpose(0, 2, 1, 3).reshape(PROMPTS * KVH, SPAN, HD)
    v_heads = values.transpose(0, 2, 1, 3).reshape(PROMPTS * KVH, SPAN, HD)
    items = jnp.arange(PROMPTS * KVH * nqb, dtype=jnp.int32)

    def attend(inputs):
        q_block, item = inputs
        pair = item // nqb
        prompt = pair // KVH
        block = item % nqb
        k_one = lax.dynamic_index_in_dim(k_heads, pair, 0, keepdims=False)
        v_one = lax.dynamic_index_in_dim(v_heads, pair, 0, keepdims=False)
        length = lax.dynamic_index_in_dim(prompt_lengths, prompt, 0, keepdims=False)
        q_pos = block * qrows + jnp.arange(qrows, dtype=jnp.int32)
        k_pos = jnp.arange(SPAN, dtype=jnp.int32)
        allowed = (k_pos[None, :] <= q_pos[:, None]) & (k_pos[None, :] < length)
        scores = jnp.einsum('qgd,kd->qgk', q_block.astype(jnp.float32), k_one.astype(jnp.float32)) * scale
        scores = jnp.where(allowed[:, None, :], scores, -jnp.inf)
        top = lax.optimization_barrier(jnp.max(scores, axis=-1, keepdims=True))
        weights = jnp.exp(scores - top)
        total = lax.optimization_barrier(jnp.sum(weights, axis=-1))
        rounded = lax.optimization_barrier(weights.astype(jnp.bfloat16)).astype(jnp.float32)
        mixed = jnp.einsum('qgk,kd->qgd', rounded, v_one.astype(jnp.float32))
        context = mixed / total[..., None]
        context = jnp.where((q_pos < length)[:, None, None], context, 0.0)
        return context.astype(jnp.bfloat16)
    outputs = lax.map(attend, (q_items, items))
    prefill_context = outputs.reshape(PROMPTS, KVH, nqb, qrows, group_size, HD).transpose(0, 2, 3, 1, 4, 5)
    prefill_context = prefill_context.reshape(PROMPTS, SPAN, HEADS * HD)
    stacked_pieces = jnp.stack([keys.reshape(PROMPTS, SPAN, KVH * HD), values.reshape(PROMPTS, SPAN, KVH * HD)], axis=2)
    block_list = stacked_pieces.reshape(PROMPTS, SHARDS, CT // BLK, BLK, 2, KVH * HD).transpose(1, 2, 0, 3, 4, 5)
    block_list = block_list.reshape(SHARDS, NB_DEV, BLK * 2 * KVH * HD)
    owners = block_owner.reshape(SHARDS, NB_DEV).astype(jnp.int32)
    earlier = jnp.tril(jnp.ones((NB_DEV, NB_DEV), jnp.int32), -1)
    same = (owners[:, :, None] == owners[:, None, :]).astype(jnp.int32)
    ranks = lax.optimization_barrier(jnp.sum(same * earlier[None], axis=2))
    target_index = jnp.arange(SHARDS, dtype=jnp.int32)
    slot_ids = jnp.arange(CAP, dtype=jnp.int32)
    choose_entries = (owners[:, None, None, :] == target_index[None, :, None, None]) & (ranks[:, None, None, :] == slot_ids[None, None, :, None])
    pool = jnp.einsum('sdci,six->dscx', choose_entries.astype(jnp.float32), block_list.astype(jnp.float32))
    kv_pool = pool.astype(jnp.bfloat16).reshape(SHARDS, SHARDS * CAP, BLK, 2, KVH * HD)
    new_pos = cache_lengths[:, None].astype(jnp.float32) + jnp.arange(STEPS, dtype=jnp.float32)[None, :]
    dq = project(decode_hidden, w_query, HEADS, query_gain, new_pos)
    dk = project(decode_hidden, w_key, KVH, key_gain, new_pos)
    dv = plain_values(decode_hidden, w_value, KVH)
    all_keys = jnp.concatenate([key_cache.reshape(ROWS, CACHE, KVH, HD), dk], axis=1)
    all_values = jnp.concatenate([value_cache.reshape(ROWS, CACHE, KVH, HD), dv], axis=1)
    qg = dq.reshape(ROWS, STEPS, KVH, group_size, HD)
    scores = jnp.einsum('rsngd,rknd->rngsk', qg.astype(jnp.float32), all_keys.astype(jnp.float32)) * scale
    slot = jnp.arange(CACHE + STEPS, dtype=jnp.int32)
    step = jnp.arange(STEPS, dtype=jnp.int32)
    allowed = jnp.where(slot[None, None, :] < CACHE, slot[None, None, :] < cache_lengths[:, None, None], slot[None, None, :] - CACHE <= step[None, :, None])
    scores = jnp.where(allowed[:, None, None], scores, -jnp.inf)
    top = lax.optimization_barrier(jnp.max(scores, axis=-1, keepdims=True))
    weights = jnp.exp(scores - top)
    total = lax.optimization_barrier(jnp.sum(weights, axis=-1))
    rounded = lax.optimization_barrier(weights.astype(jnp.bfloat16)).astype(jnp.float32)
    mixed = jnp.einsum('rngsk,rknd->rngsd', rounded, all_values.astype(jnp.float32)) / total[..., None]
    context = mixed.transpose(0, 3, 1, 2, 4).reshape(ROWS * STEPS, HEADS * HD).astype(jnp.bfloat16)
    decode_out = jnp.dot(context, w_out, preferred_element_type=jnp.float32).astype(jnp.bfloat16).reshape(ROWS, STEPS, D)
    return (prefill_context, kv_pool, decode_out)
```

```python
import numpy as np
import jax
import jax.numpy as jnp
from jax import lax
from jax.experimental import pallas as pl
from jax.experimental.pallas import tpu as pltpu
from jax.sharding import PartitionSpec as P

MESH = pl.DeviceIdType.MESH
F32 = jnp.float32
BF16 = jnp.bfloat16
I32 = jnp.int32

EPS = 1e-06
THETA = 1000000.0
HD = 128
TOK = 256
NP = 2
ROWS = NP * TOK
NH = 4
DR = 8
ST = 4
DT = DR * ST
D = 5120
CACHE = 1024
NS = 16
KCH = 1024
NKC = D // KCH
PIECE = D // 8
SM = HD**-0.5 * 1.4426950408889634

ORDER = [
    (0, 0),
    (3, 0), (1, 0), (0, 3), (0, 1),
    (2, 0), (0, 2),
    (3, 3), (1, 1), (3, 1), (1, 3),
    (3, 2), (1, 2), (2, 3), (2, 1),
    (2, 2),
]
STEP = {o: k for k, o in enumerate(ORDER)}


def rem(a, b):
    return lax.rem(a, b if a.ndim == 0 else jnp.full(a.shape, b, a.dtype))


def div(a, b):
    return lax.div(a, b if a.ndim == 0 else jnp.full(a.shape, b, a.dtype))


def nt(a, b):
    return lax.dot_general(a, b, (((1,), (1,)), ((), ())), preferred_element_type=F32)


def mm(a, b):
    return jnp.dot(a, b, preferred_element_type=F32)


def iota(shape, dim):
    return lax.broadcasted_iota(I32, shape, dim)


def norm_rope(raw, gain, cosine, sine):
    mean_sq = jnp.mean(raw * raw, axis=-1, keepdims=True)
    u = raw * lax.rsqrt(mean_sq + EPS) * gain
    return (u * cosine + pltpu.roll(u, HD // 2, 1) * sine).astype(BF16)


def kernel(
    start_ref, len_ref, owner_ref, clen_ref,
    freq_ref, cosb_ref, sinb_ref, qg_ref, kg_ref,
    x_hbm, hd_hbm, kc_hbm, vc_hbm, wq_hbm, wk_hbm, wv_hbm, wo_hbm,
    ctx_hbm, pool_hbm, dec_hbm,
    xs, hd, kc, vc, wq, wkv, wo,
    kvacc, qacc, cosf, sinf, dcos, dsin,
    G, Qs, M, L, ACC, dk, dv, dq,
    CT, CS, PI, pool, ctxs,
    PS, RS, DO,
    in_sem, out_sem, send_sem, recv_sem, tsend_sem, trecv_sem, ct_sem,
    rs_send, rs_recv, ag_send, ag_recv,
):
    g = lax.axis_index("group")
    s = lax.axis_index("seq")
    t = lax.axis_index("tp")
    X = g * 2 + rem(s, 2)
    Y = div(s, 2)
    me = g * 8 + s

    place = {}
    for dx, dy in ORDER:
        xx = rem(X + dx, 4)
        yy = rem(Y + dy, 4)
        place[dx, dy] = div(xx, 2), yy * 2 + rem(xx, 2)
    place_shard = {o: gg * 8 + ss for o, (gg, ss) in place.items()}
    num = [g * 0 + i for i in range(64)]
    tps = [rem(t + i, 8) for i in range(8)]
    tp_cols = [pl.ds(pl.multiple_of(u * PIECE, HD), PIECE) for u in tps]

    def at(dx, dy):
        return place[dx, dy]

    def shard(dx, dy):
        return place_shard[dx, dy]

    loads = []

    def load(src, dst, n):
        c = pltpu.make_async_copy(src, dst, in_sem.at[n])
        c.start()
        return c

    n = 0
    first = []
    for i in range(NKC):
        ks = pl.ds(i * KCH, KCH)
        first.append((
            load(x_hbm.at[:, ks], xs.at[pl.ds(0, ROWS), ks], n),
            load(wk_hbm.at[ks, :], wkv.at[ks, pl.ds(0, HD)], n + 1),
            load(wv_hbm.at[ks, :], wkv.at[ks, pl.ds(HD, HD)], n + 2),
        ))
        n += 3
        if i == 0:
            hd_load = load(hd_hbm, hd, n)
            n += 1
    wq_load = []
    for i in range(NKC):
        ks = pl.ds(i * KCH, KCH)
        wq_load.append(load(wq_hbm.at[ks, :], wq.at[ks, :], n))
        n += 1
    kc_load = load(kc_hbm, kc, n)
    vc_load = load(vc_hbm, vc, n + 1)
    wo_load = load(wo_hbm, wo, n + 2)

    bar = pltpu.get_barrier_semaphore()
    peers = [at(dx, dy) for dx, dy in ORDER[1:]]
    for gg, ss in peers:
        pl.semaphore_signal(bar, inc=1, device_id=(gg, ss, t), device_id_type=MESH)
    for i in range(1, 8):
        pl.semaphore_signal(bar, inc=1, device_id=(g, s, tps[i]), device_id_type=MESH)

    freq = freq_ref[...]
    sign = jnp.where(iota((1, HD), 1) < HD // 2, -1.0, 1.0).astype(F32)
    for p in range(NP):
        base = (start_ref[p] + me * TOK).astype(F32) * freq
        ca = jnp.cos(base)
        sa = jnp.sin(base) * sign
        cb = cosb_ref[...]
        sb = sinb_ref[...]
        rows = pl.ds(p * TOK, TOK)
        cosf[rows, :] = cb * ca - sb * sa
        sinf[rows, :] = cb * sa + sb * ca
    row = iota((DT, HD), 0)
    pos = rem(row, ST)
    for r in range(DR):
        pos = pos + jnp.where(div(row, ST) == r, clen_ref[r], 0)
    ang = pos.astype(F32) * freq
    dcos[...] = jnp.cos(ang)
    dsin[...] = jnp.sin(ang) * sign

    lane = iota((8, HD), 1)
    want_o = div(lane, 2)
    want_r = rem(lane, 2)
    table = jnp.full((8, HD), -1, I32)
    seen = jnp.zeros((8, HD), I32)
    for v in range(NS):
        hit = want_o == owner_ref[v % 2, v // 2]
        table = jnp.where(hit & (seen == want_r), v, table)
        seen = seen + hit.astype(I32)
    CT[me] = table

    ro = iota((HD, HD), 0)
    co = iota((HD, HD), 1)
    src = div(ro, 64) * 64 + rem(ro, 2) * 32 + div(rem(ro, 64), 2)
    PI[...] = jnp.where(co == src, 1.0, 0.0).astype(BF16)

    hd_load.wait()
    xs[pl.ds(ROWS, DT), :] = hd[...].astype(F32).reshape(DT, D).astype(BF16)

    for i in range(NKC):
        for c in first[i]:
            c.wait()
        ks = pl.ds(i * KCH, KCH)
        part = mm(xs[:, ks], wkv[ks, :])
        if i == 0:
            kvacc[...] = part
        else:
            kvacc[...] += part
    kg = kg_ref[...]
    for p in range(NP):
        rows = pl.ds(p * TOK, TOK)
        G[me, p, 0] = norm_rope(kvacc[rows, :HD], kg, cosf[rows, :], sinf[rows, :])
        G[me, p, 1] = kvacc[rows, HD:].astype(BF16)
    drows = pl.ds(ROWS, DT)
    dk[...] = norm_rope(kvacc[drows, :HD], kg, dcos[...], dsin[...])
    dv[...] = kvacc[drows, HD:].astype(BF16)

    pl.semaphore_wait(bar, len(peers) + 7)

    sends = []

    def rid(k, p, half):
        return (k * 2 + p) * 2 + half

    def send(dx, dy, p, half, to):
        k = STEP[((dx - to[0]) % 4, (dy - to[1]) % 4)]
        j = shard(dx, dy)
        ref = G.at[j, num[p]] if half is None else G.at[j, num[p], num[half]]
        gg, ss = at(*to)
        c = pltpu.make_async_remote_copy(
            src_ref=ref, dst_ref=ref,
            send_sem=send_sem.at[num[len(sends)]],
            recv_sem=recv_sem.at[num[rid(k, p, half or 0)]],
            device_id=(gg, ss, t), device_id_type=MESH,
        )
        sends.append(c)
        c.start()

    def arrive(k, p, half):
        j = shard(*ORDER[k])
        ref = G.at[j, num[p]] if half is None else G.at[j, num[p], num[half]]
        pltpu.make_async_remote_copy(
            src_ref=ref, dst_ref=ref, send_sem=send_sem.at[num[0]],
            recv_sem=recv_sem.at[num[rid(k, p, half or 0)]],
            device_id=(g, s, t), device_id_type=MESH,
        ).wait_recv()

    def flip(o, p):
        return o if p == 0 else (o[1], o[0])

    def comm(k):
        for p in range(NP):
            a, b = flip(ORDER[k], p)
            o = ORDER[k]
            if a == 2 and b == 0 or b == 2:
                arrive(k, p, 0)
                arrive(k, p, 1)
            else:
                arrive(k, p, None)
            if b == 0 and a in (1, 3):
                send(*o, p, 0 if a == 3 else 1, flip((4 - a, 0), p))
            if b == 0:
                send(*o, p, None, flip((0, 1), p))
                send(*o, p, None, flip((0, 3), p))
            if b in (1, 3):
                send(*o, p, 0 if b == 3 else 1, flip((0, 4 - b), p))

    for p in range(NP):
        for d in (1, 3):
            send(0, 0, p, None, flip((d, 0), p))
    for p in range(NP):
        for d in (1, 3):
            send(0, 0, p, None, flip((0, d), p))

    tsends = []
    for i, (dx, dy) in enumerate(ORDER[1:]):
        gg, ss = at(dx, dy)
        k = STEP[((-dx) % 4, (-dy) % 4)]
        c = pltpu.make_async_remote_copy(
            src_ref=CT.at[me], dst_ref=CT.at[me],
            send_sem=tsend_sem.at[num[i]], recv_sem=trecv_sem.at[num[k]],
            device_id=(gg, ss, t), device_id_type=MESH,
        )
        c.start()
        tsends.append(c)

    for i in range(NKC):
        wq_load[i].wait()
        ks = pl.ds(i * KCH, KCH)
        part = mm(xs[:, ks], wq[ks, :])
        if i == 0:
            qacc[...] = part
        else:
            qacc[...] += part
    qg = qg_ref[...]
    for h in range(NH):
        cols = pl.ds(h * HD, HD)
        for p in range(NP):
            rows = pl.ds(p * TOK, TOK)
            Qs[p, h] = norm_rope(qacc[rows, cols], qg, cosf[rows, :], sinf[rows, :])
        dq[:, cols] = norm_rope(qacc[drows, cols], qg, dcos[...], dsin[...])

    def attend(p, h, j, own):
        q = Qs[p, h]
        sc = nt(q, G[j, p, 0])
        if own:
            sc = jnp.where(iota((TOK, TOK), 1) <= iota((TOK, TOK), 0), sc, -1e30)
        s0 = sc[:, :HD]
        s1 = sc[:, HD:]
        top = jnp.max(jnp.maximum(s0, s1), axis=1, keepdims=True)
        if own:
            new = jnp.broadcast_to(top, (TOK, HD))
        else:
            old = M[p, h]
            new = jnp.maximum(old, top)
        mb = new * SM
        p0 = jnp.exp2(s0 * SM - mb)
        p1 = jnp.exp2(s1 * SM - mb)
        w = jnp.concatenate([p0.astype(BF16), p1.astype(BF16)], axis=1)
        o = mm(w, G[j, p, 1])
        M[p, h] = new
        if own:
            L[p, h] = p0 + p1
            ACC[p, h] = o
        else:
            alpha = jnp.exp2(old * SM - mb)
            L[p, h] = L[p, h] * alpha + (p0 + p1)
            ACC[p, h] = ACC[p, h] * alpha + o

    def blocks(j):
        rows = []
        for r in range(2):
            code = CS[j, 0, me * 2 + r]
            kb = jnp.zeros((32, HD), BF16)
            vb = jnp.zeros((32, HD), BF16)
            for v in range(NS):
                here = code == v
                span = pl.ds((v // 2) * 32, 32)
                kb = jnp.where(here, G[j, v % 2, 0, span, :], kb)
                vb = jnp.where(here, G[j, v % 2, 1, span, :], vb)
            rows += [kb, vb]
        both = jnp.concatenate(rows, axis=0)
        pool[j] = mm(PI[...], both).astype(BF16)

    for p in range(NP):
        for h in range(NH):
            attend(p, h, me, True)

    for k in (1, 2, 3, 4):
        comm(k)

    kc_load.wait()
    vc_load.wait()
    er = iota((HD, DT), 0)
    ec = iota((HD, DT), 1)
    same = div(er, 16) == div(ec, ST)
    qd = jnp.zeros((HD, HD), F32)
    for h in range(NH):
        pick = same & (rem(er, ST) == rem(ec, ST)) & (rem(div(er, ST), NH) == h)
        qd = qd + mm(jnp.where(pick, 1.0, 0.0).astype(BF16), dq[:, h * HD:(h + 1) * HD])
    qd = qd.astype(BF16)
    sn = nt(qd, dk[...])
    sn = jnp.where(same & (rem(ec, ST) <= rem(er, ST)), sn, -1e30)
    outs = []
    for r in range(DR):
        span = slice(r * 16, r * 16 + 16)
        sr = nt(qd[span], kc[r])
        sr = jnp.where(iota((16, CACHE), 1) < clen_ref[r], sr, -1e30)
        top = jnp.maximum(
            jnp.max(sr, axis=1, keepdims=True), jnp.max(sn[span], axis=1, keepdims=True)
        )
        wr = jnp.exp2((sr - top) * SM)
        wn = jnp.exp2((sn[span] - top) * SM)
        total = jnp.sum(wr, axis=1, keepdims=True) + jnp.sum(wn, axis=1, keepdims=True)
        mixed = mm(wr.astype(BF16), vc[r]) + mm(wn.astype(BF16), dv[...])
        outs.append(mixed / total)
    cd = jnp.concatenate(outs, axis=0).astype(BF16)
    tr = iota((DT, HD), 0)
    tc = iota((DT, HD), 1)
    heads = []
    for h in range(NH):
        pick = (div(tc, 16) == div(tr, ST)) & (rem(tc, ST) == rem(tr, ST)) & (rem(div(tc, ST), NH) == h)
        heads.append(mm(jnp.where(pick, 1.0, 0.0).astype(BF16), cd).astype(BF16))
    dctx = jnp.concatenate(heads, axis=1)
    wo_load.wait()
    for i in range(8):
        PS[i] = mm(dctx, wo[:, i * PIECE:(i + 1) * PIECE]).astype(BF16)
    rsends = []
    for i in range(1, 8):
        to = tps[i]
        c = pltpu.make_async_remote_copy(
            src_ref=PS.at[to], dst_ref=RS.at[t],
            send_sem=rs_send.at[num[i]], recv_sem=rs_recv.at[num[8 - i]],
            device_id=(g, s, to), device_id_type=MESH,
        )
        c.start()
        rsends.append(c)

    for k in range(1, NS):
        j = shard(*ORDER[k])
        pltpu.make_async_remote_copy(
            src_ref=CT.at[j], dst_ref=CT.at[j], send_sem=tsend_sem.at[num[0]],
            recv_sem=trecv_sem.at[num[k]], device_id=(g, s, t), device_id_type=MESH,
        ).wait_recv()
    ctc = pltpu.make_async_copy(CT, CS, ct_sem)
    ctc.start()
    ctc.wait()
    blocks(me)

    asends = []
    mine = tp_cols[0]

    def reduce():
        total = PS[t].astype(F32)
        for i in range(1, 8):
            frm = tps[i]
            pltpu.make_async_remote_copy(
                src_ref=PS.at[frm], dst_ref=RS.at[frm], send_sem=rs_send.at[num[0]],
                recv_sem=rs_recv.at[num[i]], device_id=(g, s, t), device_id_type=MESH,
            ).wait_recv()
            total = total + RS[frm].astype(F32)
        DO[:, mine] = total.astype(BF16)
        for i in range(1, 8):
            c = pltpu.make_async_remote_copy(
                src_ref=DO.at[:, mine], dst_ref=DO.at[:, mine],
                send_sem=ag_send.at[num[i]], recv_sem=ag_recv.at[num[8 - i]],
                device_id=(g, s, tps[i]), device_id_type=MESH,
            )
            c.start()
            asends.append(c)

    @pl.loop(1, NS)
    def _(kk):
        j = 0
        for k in range(1, NS):
            j = j + jnp.where(kk == k, shard(*ORDER[k]), 0)
            if k > 4:
                @pl.when(kk == k)
                def _():
                    comm(k)

        @pl.when(kk == 5)
        def _():
            reduce()

        @pl.when(j < me)
        def _():
            for p in range(NP):
                for h in range(NH):
                    attend(p, h, j, False)
        blocks(j)

    pool_out = pltpu.make_async_copy(pool, pool_hbm, out_sem.at[0])
    pool_out.start()

    for i in range(1, 8):
        frm = tps[i]
        cols = tp_cols[i]
        pltpu.make_async_remote_copy(
            src_ref=DO.at[:, cols], dst_ref=DO.at[:, cols], send_sem=ag_send.at[num[0]],
            recv_sem=ag_recv.at[num[i]], device_id=(g, s, t), device_id_type=MESH,
        ).wait_recv()
    dec_out = pltpu.make_async_copy(DO, dec_hbm, out_sem.at[1])
    dec_out.start()

    for p in range(NP):
        tok = me * TOK + iota((TOK, HD), 0)
        keep = tok < len_ref[p]
        for h in range(NH):
            total = jnp.sum(L[p, h], axis=1, keepdims=True)
            out = jnp.where(keep, ACC[p, h] / total, 0.0)
            ctxs[pl.ds(p * TOK, TOK), pl.ds(h * HD, HD)] = out.astype(BF16)
    ctx_out = pltpu.make_async_copy(ctxs, ctx_hbm, out_sem.at[2])
    ctx_out.start()
    for c in sends + tsends + rsends + asends:
        c.wait_send()
    pool_out.wait()
    dec_out.wait()
    ctx_out.wait()


def tables():
    freq = THETA ** (-np.arange(HD // 2, dtype=np.float64) * 2.0 / HD)
    ang = np.arange(TOK, dtype=np.float64)[:, None] * freq[None, :]
    cosb = np.concatenate([np.cos(ang), np.cos(ang)], axis=1).astype(np.float32)
    sinb = np.concatenate([-np.sin(ang), np.sin(ang)], axis=1).astype(np.float32)
    freq = np.concatenate([freq, freq])[None, :].astype(np.float32)
    return freq, cosb, sinb


def per_device(
    prompt_tokens, prompt_lengths, prompt_token_start, block_owner, decode_hidden,
    cache_lengths, key_cache, value_cache, w_query, w_key, w_value, w_out,
    query_gain, key_gain,
):
    freq, cosb, sinb = (jnp.asarray(a) for a in tables())
    vm = pl.BlockSpec(memory_space=pltpu.VMEM)
    sm = pl.BlockSpec(memory_space=pltpu.SMEM)
    hbm = pl.BlockSpec(memory_space=pl.ANY)
    V = pltpu.VMEM
    ctx, pool, dec = pl.pallas_call(
        kernel,
        out_shape=(
            jax.ShapeDtypeStruct((ROWS, NH * HD), BF16),
            jax.ShapeDtypeStruct((NS, HD, HD), BF16),
            jax.ShapeDtypeStruct((DT, D), BF16),
        ),
        in_specs=[sm] * 4 + [vm] * 5 + [hbm] * 8,
        out_specs=(hbm, hbm, hbm),
        scratch_shapes=[
            V((ROWS + DT, D), BF16),
            V((DR, ST, D), BF16),
            V((DR, CACHE, HD), BF16),
            V((DR, CACHE, HD), BF16),
            V((D, NH * HD), BF16),
            V((D, 2 * HD), BF16),
            V((NH * HD, D), BF16),
            V((ROWS + DT, 2 * HD), F32),
            V((ROWS + DT, NH * HD), F32),
            V((ROWS, HD), F32),
            V((ROWS, HD), F32),
            V((DT, HD), F32),
            V((DT, HD), F32),
            V((NS, NP, 2, TOK, HD), BF16),
            V((NP, NH, TOK, HD), BF16),
            V((NP, NH, TOK, HD), F32),
            V((NP, NH, TOK, HD), F32),
            V((NP, NH, TOK, HD), F32),
            V((DT, HD), BF16),
            V((DT, HD), BF16),
            V((DT, NH * HD), BF16),
            V((NS, 8, HD), I32),
            pltpu.SMEM((NS, 8, HD), I32),
            V((HD, HD), BF16),
            V((NS, HD, HD), BF16),
            V((ROWS, NH * HD), BF16),
            V((8, DT, PIECE), BF16),
            V((8, DT, PIECE), BF16),
            V((DT, D), BF16),
            pltpu.SemaphoreType.DMA((32,)),
            pltpu.SemaphoreType.DMA((3,)),
            pltpu.SemaphoreType.DMA((64,)),
            pltpu.SemaphoreType.DMA((64,)),
            pltpu.SemaphoreType.DMA((16,)),
            pltpu.SemaphoreType.DMA((16,)),
            pltpu.SemaphoreType.DMA,
            pltpu.SemaphoreType.DMA((8,)),
            pltpu.SemaphoreType.DMA((8,)),
            pltpu.SemaphoreType.DMA((8,)),
            pltpu.SemaphoreType.DMA((8,)),
        ],
        compiler_params=pltpu.CompilerParams(
            collective_id=0, has_side_effects=True, vmem_limit_bytes=58 * 1024 * 1024
        ),
        name="split_attention",
    )(
        prompt_token_start, prompt_lengths,
        block_owner.transpose(1, 2, 0).reshape(NP, 8), cache_lengths,
        freq, cosb, sinb,
        query_gain.reshape(1, HD), key_gain.reshape(1, HD),
        prompt_tokens.reshape(ROWS, D), decode_hidden, key_cache, value_cache,
        w_query, w_key, w_value, w_out,
    )
    return (
        ctx.reshape(NP, TOK, NH * HD),
        pool.reshape(1, 2 * NS, 32, 2, HD),
        dec.reshape(DR, ST, D),
    )


def solution(mesh):
    placed = (
        P(None, ("group", "seq"), None),
        P(),
        P(),
        P(("group", "seq"), None, None),
        P(("group", "seq"), None, None),
        P(("group", "seq")),
        P(("group", "seq"), None, "tp"),
        P(("group", "seq"), None, "tp"),
        P(None, "tp"),
        P(None, "tp"),
        P(None, "tp"),
        P("tp", None),
        P(),
        P(),
    )
    return jax.shard_map(
        per_device,
        mesh=mesh,
        in_specs=placed,
        out_specs=(
            P(None, ("group", "seq"), "tp"),
            P(("group", "seq"), None, None, None, "tp"),
            P(("group", "seq"), None, None),
        ),
        check_vma=False,
    )
```

```python
import numpy as np
import jax
import jax.numpy as jnp
from jax import lax
from jax.experimental import pallas as pl
from jax.experimental.pallas import tpu as pltpu
from jax.sharding import PartitionSpec as P

MESH = pl.DeviceIdType.MESH
F32 = jnp.float32
BF16 = jnp.bfloat16
I32 = jnp.int32

EPS = 1e-06
THETA = 1000000.0
HD = 128
TOK = 256
NP = 2
ROWS = NP * TOK
NH = 4
DR = 8
ST = 4
DT = DR * ST
D = 5120
CACHE = 1024
NS = 16
CH = 2 * TOK + 16
KCH = 1024
NKC = D // KCH
PIECE = D // 8
SM = HD**-0.5 * 1.4426950408889634

ORDER = [
    (0, 0),
    (3, 0), (1, 0), (0, 3), (0, 1),
    (2, 0), (0, 2),
    (3, 3), (1, 1), (3, 1), (1, 3),
    (3, 2), (1, 2), (2, 3), (2, 1),
    (2, 2),
]
STEP = {o: k for k, o in enumerate(ORDER)}
LATER = {
    3: ((7, 0), (8, 0), (7, 1), (8, 1)),
    4: ((9, 0), (10, 0), (9, 1), (10, 1)),
    5: ((5, 1),),
    6: ((6, 0),),
    8: ((13, 0), (14, 0), (11, 1), (12, 1)),
    11: ((11, 0), (12, 0)),
    13: ((13, 1), (14, 1)),
    15: ((15, 0), (15, 1)),
}


def rem(a, b):
    return lax.rem(a, b) if a.ndim == 0 else a & (b - 1)


def div(a, b):
    return lax.div(a, b) if a.ndim == 0 else lax.shift_right_logical(a, jnp.full(a.shape, b.bit_length() - 1, a.dtype))


def nt(a, b):
    return lax.dot_general(a, b, (((1,), (1,)), ((), ())), preferred_element_type=F32)


def mm(a, b):
    return jnp.dot(a, b, preferred_element_type=F32)


def iota(shape, dim):
    return lax.broadcasted_iota(I32, shape, dim)


def norm_rope(raw, gain, cosine, sine):
    mean_sq = mm((raw * raw).astype(BF16), jnp.full((HD, HD), 1.0 / HD, BF16))
    u = raw * lax.rsqrt(mean_sq + EPS) * gain
    return (u * cosine + pltpu.roll(u, HD // 2, 1) * sine).astype(BF16)


def kernel(
    start_ref, len_ref, owner_ref, clen_ref,
    tab_hbm, qg_hbm, kg_hbm,
    x_hbm, hd_hbm, kc_hbm, vc_hbm, wq_hbm, wk_hbm, wv_hbm, wo_hbm,
    ctx_hbm, pool_hbm, dec_hbm,
    xs, hd, kc, vc, wq, wkv, wo,
    kvacc, qacc, cosf, sinf, dcos, dsin,
    G, Qs, M, L, ACC, dk, dv, dq,
    tab, gains, PI, NUM, pool, ctxs,
    PS, RS, DO,
    in_sem, out_sem, send_sem, recv_sem,
    rs_send, rs_recv, ag_send, ag_recv,
):
    g = lax.axis_index("group")
    s = lax.axis_index("seq")
    t = lax.axis_index("tp")
    X = g * 2 + rem(s, 2)
    Y = div(s, 2)
    me = g * 8 + s

    place = {}
    for dx, dy in ORDER:
        xx = rem(X + dx, 4)
        yy = rem(Y + dy, 4)
        place[dx, dy] = div(xx, 2), yy * 2 + rem(xx, 2)
    place_shard = {o: gg * 8 + ss for o, (gg, ss) in place.items()}
    num = [g * 0 + i for i in range(64)]
    tps = [rem(t + i, 8) for i in range(8)]
    tp_cols = [pl.ds(pl.multiple_of(u * PIECE, HD), PIECE) for u in tps]

    def at(dx, dy):
        return place[dx, dy]

    def shard(dx, dy):
        return place_shard[dx, dy]

    def load(src, dst, n, now=True):
        c = pltpu.make_async_copy(src, dst, in_sem.at[n])
        if now:
            c.start()
        return c

    n = 0
    first = []
    for i in range(NKC):
        ks = pl.ds(i * KCH, KCH)
        first.append((
            load(x_hbm.at[:, ks], xs.at[pl.ds(0, ROWS), ks], n),
            load(wk_hbm.at[ks, :], wkv.at[ks, pl.ds(0, HD)], n + 1),
            load(wv_hbm.at[ks, :], wkv.at[ks, pl.ds(HD, HD)], n + 2),
        ))
        n += 3
        if i == 0:
            hd_load = load(hd_hbm, hd, n)
            small = (
                load(tab_hbm, tab, n + 1),
                load(qg_hbm, gains.at[0], n + 2),
                load(kg_hbm, gains.at[1], n + 3),
            )
            n += 4
    wq_load = []
    for i in range(NKC):
        ks = pl.ds(i * KCH, KCH)
        wq_load.append(load(wq_hbm.at[ks, :], wq.at[ks, :], n, False))
        n += 1
    kc_load = load(kc_hbm, kc, n, False)
    vc_load = load(vc_hbm, vc, n + 1, False)
    wo_load = load(wo_hbm, wo, n + 2, False)

    bar = pltpu.get_barrier_semaphore()
    for o in ((1, 0), (3, 0), (0, 1), (0, 3)):
        gg, ss = at(*o)
        pl.semaphore_signal(bar, inc=1, device_id=(gg, ss, t), device_id_type=MESH)
    for i in range(1, 8):
        pl.semaphore_signal(bar, inc=1, device_id=(g, s, tps[i]), device_id_type=MESH)

    lane = iota((16, HD), 1)
    want_o = div(lane, 2)
    want_r = rem(lane, 2)
    table = jnp.full((16, HD), -1, I32)
    seen = jnp.zeros((16, HD), I32)
    for v in range(NS):
        hit = want_o == owner_ref[v % 2, v // 2]
        table = jnp.where(hit & (seen == want_r), v, table)
        seen = seen + hit.astype(I32)
    for p in range(NP):
        G[me, p, pl.ds(2 * TOK, 16), :] = table.astype(F32).astype(BF16)

    for c in small:
        c.wait()
    freq = tab[pl.ds(2 * TOK, 1), :]
    sign = jnp.where(iota((1, HD), 1) < HD // 2, -1.0, 1.0).astype(F32)
    for p in range(NP):
        base = (start_ref[p] + me * TOK).astype(F32) * freq
        ca = jnp.cos(base)
        sa = jnp.sin(base) * sign
        cb = tab[pl.ds(0, TOK), :]
        sb = tab[pl.ds(TOK, TOK), :]
        rows = pl.ds(p * TOK, TOK)
        cosf[rows, :] = cb * ca - sb * sa
        sinf[rows, :] = cb * sa + sb * ca
    row = iota((DT, HD), 0)
    pos = rem(row, ST)
    for r in range(DR):
        pos = pos + jnp.where(div(row, ST) == r, clen_ref[r], 0)
    ang = pos.astype(F32) * freq
    dcos[...] = jnp.cos(ang)
    dsin[...] = jnp.sin(ang) * sign

    hd_load.wait()
    xs[pl.ds(ROWS, DT), :] = hd[...].astype(F32).reshape(DT, D).astype(BF16)

    for i in range(NKC):
        for c in first[i]:
            c.wait()
        if i >= NKC - 2:
            for c in wq_load[:2] if i == NKC - 2 else wq_load[2:]:
                c.start()
        ks = pl.ds(i * KCH, KCH)
        part = mm(xs[:, ks], wkv[ks, :])
        if i == 0:
            kvacc[...] = part
        else:
            kvacc[...] += part
    kg = gains[1]
    for p in range(NP):
        rows = pl.ds(p * TOK, TOK)
        G[me, p, pl.ds(0, TOK), :] = norm_rope(kvacc[rows, :HD], kg, cosf[rows, :], sinf[rows, :])
        G[me, p, pl.ds(TOK, TOK), :] = kvacc[rows, HD:].astype(BF16)
    drows = pl.ds(ROWS, DT)
    dk[...] = norm_rope(kvacc[drows, :HD], kg, dcos[...], dsin[...])
    dv[...] = kvacc[drows, HD:].astype(BF16)

    def query_part(i):
        wq_load[i].wait()
        ks = pl.ds(i * KCH, KCH)
        part = mm(xs[:, ks], wq[ks, :])
        if i == 0:
            qacc[...] = part
        else:
            qacc[...] += part

    query_part(0)
    query_part(1)
    kc_load.start()
    vc_load.start()

    pl.semaphore_wait(bar, 4 + 7)

    sends = []

    def part_of(j, p, half):
        if half is None:
            return G.at[j, num[p]]
        return G.at[j, num[p], pl.ds(0, TOK) if half == 0 else pl.ds(TOK, CH - TOK)]

    def rid(k, p, half):
        return (k * 2 + p) * 2 + half

    def send(dx, dy, p, half, to):
        k = STEP[((dx - to[0]) % 4, (dy - to[1]) % 4)]
        j = shard(dx, dy)
        ref = part_of(j, p, half)
        gg, ss = at(*to)
        c = pltpu.make_async_remote_copy(
            src_ref=ref, dst_ref=ref,
            send_sem=send_sem.at[num[len(sends)]],
            recv_sem=recv_sem.at[num[rid(k, p, half or 0)]],
            device_id=(gg, ss, t), device_id_type=MESH,
        )
        sends.append(c)
        c.start()

    def arrive(k, p, half):
        j = shard(*ORDER[k])
        ref = part_of(j, p, half)
        pltpu.make_async_remote_copy(
            src_ref=ref, dst_ref=ref, send_sem=send_sem.at[num[0]],
            recv_sem=recv_sem.at[num[rid(k, p, half or 0)]],
            device_id=(g, s, t), device_id_type=MESH,
        ).wait_recv()

    def flip(o, p):
        return o if p == 0 else (o[1], o[0])

    def comm(k, p):
        a, b = flip(ORDER[k], p)
        o = ORDER[k]
        if a == 2 and b == 0 or b == 2:
            arrive(k, p, 0)
            arrive(k, p, 1)
        else:
            arrive(k, p, None)
        if b == 0 and a in (1, 3):
            send(*o, p, 0 if a == 3 else 1, flip((4 - a, 0), p))
        if b == 0:
            send(*o, p, None, flip((0, 1), p))
            send(*o, p, None, flip((0, 3), p))
        if b in (1, 3):
            send(*o, p, 0 if b == 3 else 1, flip((0, 4 - b), p))

    for p in range(NP):
        for d in (1, 3):
            send(0, 0, p, None, flip((d, 0), p))
    for p in range(NP):
        for d in (1, 3):
            send(0, 0, p, None, flip((0, d), p))

    ro = iota((HD, 4 * TOK), 0)
    co = iota((HD, 4 * TOK), 1)
    same_row = (rem(ro, 2) == rem(div(co, TOK), 2)) & (div(rem(ro, 64), 2) == rem(co, 32))
    PI[...] = jnp.where(same_row, 1.0, 0.0).astype(BF16)
    col = iota((16, 4 * TOK), 1)
    number = rem(div(col, 32), 8) * 2 + div(col, 2 * TOK)
    NUM[...] = number.astype(F32)

    for i in range(2, NKC):
        query_part(i)
        if i == 3:
            wo_load.start()
    qg = gains[0]
    for h in range(NH):
        cols = pl.ds(h * HD, HD)
        for p in range(NP):
            rows = pl.ds(p * TOK, TOK)
            Qs[p, h] = norm_rope(qacc[rows, cols], qg, cosf[rows, :], sinf[rows, :])
        dq[:, cols] = norm_rope(qacc[drows, cols], qg, dcos[...], dsin[...])

    bodies = [(p, h) for p in range(NP) for h in range(NH)]

    def attend(j, own):
        def scores(p, h):
            sc = nt(Qs[p, h], G[j, p, pl.ds(0, TOK), :])
            if own:
                sc = jnp.where(iota((TOK, TOK), 1) <= iota((TOK, TOK), 0), sc, -1e30)
            return sc

        def soft(p, h, sc):
            s0 = sc[:, :HD]
            s1 = sc[:, HD:]
            top = jnp.max(jnp.maximum(s0, s1), axis=1, keepdims=True)
            if own:
                new = jnp.broadcast_to(top, (TOK, HD))
            else:
                old = M[p, h]
                new = jnp.maximum(old, top)
            mb = new * SM
            p0 = jnp.exp2(s0 * SM - mb)
            p1 = jnp.exp2(s1 * SM - mb)
            M[p, h] = new
            if own:
                L[p, h] = p0 + p1
                alpha = None
            else:
                alpha = jnp.exp2(old * SM - mb)
                L[p, h] = L[p, h] * alpha + (p0 + p1)
            return jnp.concatenate([p0.astype(BF16), p1.astype(BF16)], axis=1), alpha

        def mix(p, h, w, alpha):
            o = mm(w, G[j, p, pl.ds(TOK, TOK), :])
            ACC[p, h] = o if own else ACC[p, h] * alpha + o

        sc = scores(*bodies[0])
        waiting = None
        for n, b in enumerate(bodies):
            after = scores(*bodies[n + 1]) if n + 1 < len(bodies) else None
            if waiting is not None:
                mix(*waiting)
            waiting = (*b, *soft(*b, sc))
            sc = after
        mix(*waiting)

    def blocks(j):
        row = G[j, 0, pl.ds(2 * TOK, 16), :].astype(F32)
        number = NUM[...]
        picks = []
        for r in range(2):
            code = jnp.sum(jnp.where(lane == me * 2 + r, row, 0.0), axis=1, keepdims=True)
            picks.append(jnp.where(code == number, 1.0, 0.0).astype(BF16))
        for r in range(2):
            half = pl.ds(r * 64, 64)
            pick = PI[half, :] * jnp.concatenate([picks[r]] * 4, axis=0)
            out = mm(pick[:, : 2 * TOK], G[j, 0, pl.ds(0, 2 * TOK), :])
            out += mm(pick[:, 2 * TOK :], G[j, 1, pl.ds(0, 2 * TOK), :])
            pool[j, half, :] = out.astype(BF16)

    for k, p in ((1, 0), (2, 0), (3, 1), (4, 1)):
        comm(k, p)

    attend(me, True)

    kc_load.wait()
    vc_load.wait()
    er = iota((HD, DT), 0)
    ec = iota((HD, DT), 1)
    same = div(er, 16) == div(ec, ST)
    qd = jnp.zeros((HD, HD), F32)
    for h in range(NH):
        pick = same & (rem(er, ST) == rem(ec, ST)) & (rem(div(er, ST), NH) == h)
        qd = qd + mm(jnp.where(pick, 1.0, 0.0).astype(BF16), dq[:, h * HD:(h + 1) * HD])
    qd = qd.astype(BF16)
    sn = nt(qd, dk[...])
    sn = jnp.where(same & (rem(ec, ST) <= rem(er, ST)), sn, -1e30)
    outs = []
    for r in range(DR):
        span = slice(r * 16, r * 16 + 16)
        sr = nt(qd[span], kc[r])
        sr = jnp.where(iota((16, CACHE), 1) < clen_ref[r], sr, -1e30)
        top = jnp.maximum(
            jnp.max(sr, axis=1, keepdims=True), jnp.max(sn[span], axis=1, keepdims=True)
        )
        wr = jnp.exp2((sr - top) * SM)
        wn = jnp.exp2((sn[span] - top) * SM)
        total = jnp.sum(wr, axis=1, keepdims=True) + jnp.sum(wn, axis=1, keepdims=True)
        mixed = mm(wr.astype(BF16), vc[r]) + mm(wn.astype(BF16), dv[...])
        outs.append(mixed / total)
    cd = jnp.concatenate(outs, axis=0).astype(BF16)
    for k, p in ((3, 0), (4, 0), (1, 1), (2, 1)):
        comm(k, p)
    tr = iota((DT, HD), 0)
    tc = iota((DT, HD), 1)
    heads = []
    for h in range(NH):
        pick = (div(tc, 16) == div(tr, ST)) & (rem(tc, ST) == rem(tr, ST)) & (rem(div(tc, ST), NH) == h)
        heads.append(mm(jnp.where(pick, 1.0, 0.0).astype(BF16), cd).astype(BF16))
    dctx = jnp.concatenate(heads, axis=1)
    wo_load.wait()
    for i in range(8):
        PS[i] = mm(dctx, wo[:, i * PIECE:(i + 1) * PIECE]).astype(BF16)
    rsends = []
    for i in range(1, 8):
        to = tps[i]
        c = pltpu.make_async_remote_copy(
            src_ref=PS.at[to], dst_ref=RS.at[t],
            send_sem=rs_send.at[num[i]], recv_sem=rs_recv.at[num[8 - i]],
            device_id=(g, s, to), device_id_type=MESH,
        )
        c.start()
        rsends.append(c)

    for k, p in ((5, 0), (6, 1)):
        comm(k, p)

    asends = []
    mine = tp_cols[0]

    def reduce():
        total = PS[t].astype(F32)
        for i in range(1, 8):
            frm = tps[i]
            pltpu.make_async_remote_copy(
                src_ref=PS.at[frm], dst_ref=RS.at[frm], send_sem=rs_send.at[num[0]],
                recv_sem=rs_recv.at[num[i]], device_id=(g, s, t), device_id_type=MESH,
            ).wait_recv()
            total = total + RS[frm].astype(F32)
        DO[:, :, mine] = total.reshape(DR, ST, PIECE).astype(BF16)
        for i in range(1, 8):
            c = pltpu.make_async_remote_copy(
                src_ref=DO.at[:, :, mine], dst_ref=DO.at[:, :, mine],
                send_sem=ag_send.at[num[i]], recv_sem=ag_recv.at[num[8 - i]],
                device_id=(g, s, tps[i]), device_id_type=MESH,
            )
            c.start()
            asends.append(c)

    @pl.loop(1, NS)
    def _(kk):
        j = 0
        for k in range(1, NS):
            j = j + jnp.where(kk == k, shard(*ORDER[k]), 0)

        for when, events in LATER.items():
            @pl.when(kk == when)
            def _():
                for k, p in events:
                    comm(k, p)

        @pl.when(kk == 7)
        def _():
            reduce()

        @pl.when(j < me)
        def _():
            attend(j, False)

        for when in (4, 8, 12):
            @pl.when(kk == when)
            def _():
                for k in range(when - 4, when):
                    blocks(shard(*ORDER[k]))

    for k in range(12, NS):
        blocks(shard(*ORDER[k]))
    pool_out = pltpu.make_async_copy(pool, pool_hbm, out_sem.at[0])
    pool_out.start()
    for i in range(1, 8):
        cols = tp_cols[i]
        pltpu.make_async_remote_copy(
            src_ref=DO.at[:, :, cols], dst_ref=DO.at[:, :, cols], send_sem=ag_send.at[num[0]],
            recv_sem=ag_recv.at[num[i]], device_id=(g, s, t), device_id_type=MESH,
        ).wait_recv()
    dec_out = pltpu.make_async_copy(DO, dec_hbm, out_sem.at[1])
    dec_out.start()

    for p in range(NP):
        tok = me * TOK + iota((TOK, HD), 0)
        keep = tok < len_ref[p]
        for h in range(NH):
            total = jnp.sum(L[p, h], axis=1, keepdims=True)
            out = jnp.where(keep, ACC[p, h] / total, 0.0)
            ctxs[pl.ds(p * TOK, TOK), pl.ds(h * HD, HD)] = out.astype(BF16)
    ctx_out = pltpu.make_async_copy(ctxs, ctx_hbm, out_sem.at[2])
    ctx_out.start()
    for c in sends + rsends + asends:
        c.wait_send()
    pool_out.wait()
    dec_out.wait()
    ctx_out.wait()


def deliver(ctx_in, pool_in, dec_in, ctx, pool, dec, sem):
    copies = []
    for i, (a, b) in enumerate(((ctx_in, ctx), (pool_in, pool), (dec_in, dec))):
        c = pltpu.make_async_copy(a, b, sem.at[i])
        c.start()
        copies.append(c)
    for c in copies:
        c.wait()


def tables():
    freq = THETA ** (-np.arange(HD // 2, dtype=np.float64) * 2.0 / HD)
    ang = np.arange(TOK, dtype=np.float64)[:, None] * freq[None, :]
    tab = np.zeros((2 * TOK + 8, HD), np.float32)
    tab[:TOK] = np.concatenate([np.cos(ang), np.cos(ang)], axis=1)
    tab[TOK : 2 * TOK] = np.concatenate([-np.sin(ang), np.sin(ang)], axis=1)
    tab[2 * TOK] = np.concatenate([freq, freq])
    return tab


def per_device(
    prompt_tokens, prompt_lengths, prompt_token_start, block_owner, decode_hidden,
    cache_lengths, key_cache, value_cache, w_query, w_key, w_value, w_out,
    query_gain, key_gain,
):
    sm = pl.BlockSpec(memory_space=pltpu.SMEM)
    hbm = pl.BlockSpec(memory_space=pl.ANY)
    V = pltpu.VMEM
    ctx, pool, dec = pl.pallas_call(
        kernel,
        out_shape=(
            jax.ShapeDtypeStruct((ROWS, NH * HD), BF16),
            jax.ShapeDtypeStruct((NS, HD, HD), BF16),
            jax.ShapeDtypeStruct((DR, ST, D), BF16),
        ),
        in_specs=[sm] * 4 + [hbm] * 11,
        out_specs=(hbm, hbm, hbm),
        scratch_shapes=[
            V((ROWS + DT, D), BF16),
            V((DR, ST, D), BF16),
            V((DR, CACHE, HD), BF16),
            V((DR, CACHE, HD), BF16),
            V((D, NH * HD), BF16),
            V((D, 2 * HD), BF16),
            V((NH * HD, D), BF16),
            V((ROWS + DT, 2 * HD), F32),
            V((ROWS + DT, NH * HD), F32),
            V((ROWS, HD), F32),
            V((ROWS, HD), F32),
            V((DT, HD), F32),
            V((DT, HD), F32),
            V((NS, NP, CH, HD), BF16),
            V((NP, NH, TOK, HD), BF16),
            V((NP, NH, TOK, HD), F32),
            V((NP, NH, TOK, HD), F32),
            V((NP, NH, TOK, HD), F32),
            V((DT, HD), BF16),
            V((DT, HD), BF16),
            V((DT, NH * HD), BF16),
            V((2 * TOK + 8, HD), F32),
            V((2, 1, HD), F32),
            V((HD, 4 * TOK), BF16),
            V((16, 4 * TOK), F32),
            V((NS, HD, HD), BF16),
            V((ROWS, NH * HD), BF16),
            V((8, DT, PIECE), BF16),
            V((8, DT, PIECE), BF16),
            V((DR, ST, D), BF16),
            pltpu.SemaphoreType.DMA((32,)),
            pltpu.SemaphoreType.DMA((3,)),
            pltpu.SemaphoreType.DMA((64,)),
            pltpu.SemaphoreType.DMA((64,)),
            pltpu.SemaphoreType.DMA((8,)),
            pltpu.SemaphoreType.DMA((8,)),
            pltpu.SemaphoreType.DMA((8,)),
            pltpu.SemaphoreType.DMA((8,)),
        ],
        compiler_params=pltpu.CompilerParams(
            collective_id=0, has_side_effects=True, vmem_limit_bytes=58 * 1024 * 1024
        ),
        name="split_attention",
    )(
        prompt_token_start, prompt_lengths,
        block_owner.transpose(1, 2, 0).reshape(NP, 8), cache_lengths,
        jnp.asarray(tables()),
        query_gain.reshape(1, HD), key_gain.reshape(1, HD),
        prompt_tokens.reshape(ROWS, D), decode_hidden, key_cache, value_cache,
        w_query, w_key, w_value, w_out,
    )
    ctx, pool, dec = pl.pallas_call(
        deliver,
        out_shape=(
            jax.ShapeDtypeStruct((ROWS, NH * HD), BF16),
            jax.ShapeDtypeStruct((NS, HD, HD), BF16),
            jax.ShapeDtypeStruct((DR, ST, D), BF16),
        ),
        in_specs=[pl.BlockSpec(memory_space=pltpu.VMEM)] * 3,
        out_specs=(hbm, hbm, hbm),
        scratch_shapes=[pltpu.SemaphoreType.DMA((3,))],
        name="deliver",
    )(ctx, pool, dec)
    return (
        ctx.reshape(NP, TOK, NH * HD),
        pool.reshape(1, 2 * NS, 32, 2, HD),
        dec,
    )


def solution(mesh):
    placed = (
        P(None, ("group", "seq"), None),
        P(),
        P(),
        P(("group", "seq"), None, None),
        P(("group", "seq"), None, None),
        P(("group", "seq")),
        P(("group", "seq"), None, "tp"),
        P(("group", "seq"), None, "tp"),
        P(None, "tp"),
        P(None, "tp"),
        P(None, "tp"),
        P("tp", None),
        P(),
        P(),
    )
    return jax.shard_map(
        per_device,
        mesh=mesh,
        in_specs=placed,
        out_specs=(
            P(None, ("group", "seq"), "tp"),
            P(("group", "seq"), None, None, None, "tp"),
            P(("group", "seq"), None, None),
        ),
        check_vma=False,
    )
```

```python
import numpy as np
import jax
import jax.numpy as jnp
from jax import lax
from jax.experimental import pallas as pl
from jax.experimental.pallas import tpu as pltpu
from jax.sharding import PartitionSpec as P

MESH = pl.DeviceIdType.MESH
F32 = jnp.float32
BF16 = jnp.bfloat16
I32 = jnp.int32

EPS = 1e-06
THETA = 1000000.0
HD = 128
TOK = 256
NP = 2
ROWS = NP * TOK
NH = 4
DR = 8
ST = 4
DT = DR * ST
D = 5120
CACHE = 1024
NS = 16
CH = 2 * TOK + 16
KCH = 1024
NKC = D // KCH
PIECE = D // 8
SM = HD**-0.5 * 1.4426950408889634

ORDER = [
    (0, 0),
    (3, 0), (1, 0), (0, 3), (0, 1),
    (2, 0), (0, 2),
    (3, 3), (1, 1), (3, 1), (1, 3),
    (3, 2), (1, 2), (2, 3), (2, 1),
    (2, 2),
]
STEP = {o: k for k, o in enumerate(ORDER)}
LATER = {
    2: ((7, 0), (8, 0), (7, 1), (8, 1)),
    3: ((9, 0), (10, 0), (9, 1), (10, 1), (5, 1), (6, 0)),
    4: ((13, 0), (14, 0), (11, 1), (12, 1)),
    6: ((11, 0), (12, 0)),
    7: ((13, 1), (14, 1)),
    8: ((15, 0), (15, 1)),
}
BLOCKS = {3: range(0, 4), 5: range(4, 8), 6: range(8, 11), 8: range(11, 15)}


def rem(a, b):
    return lax.rem(a, b) if a.ndim == 0 else a & (b - 1)


def div(a, b):
    return lax.div(a, b) if a.ndim == 0 else lax.shift_right_logical(a, jnp.full(a.shape, b.bit_length() - 1, a.dtype))


def nt(a, b):
    return lax.dot_general(a, b, (((1,), (1,)), ((), ())), preferred_element_type=F32)


def mm(a, b):
    return jnp.dot(a, b, preferred_element_type=F32)


def iota(shape, dim):
    return lax.broadcasted_iota(I32, shape, dim)


def norm_rope(raw, gain, cosine, sine):
    mean_sq = mm((raw * raw).astype(BF16), jnp.full((HD, HD), 1.0 / HD, BF16))
    u = raw * lax.rsqrt(mean_sq + EPS) * gain
    return (u * cosine + pltpu.roll(u, HD // 2, 1) * sine).astype(BF16)


def kernel(
    start_ref, len_ref, owner_ref, clen_ref,
    tab_hbm, qg_hbm, kg_hbm,
    x_hbm, hd_hbm, kc_hbm, vc_hbm, wq_hbm, wk_hbm, wv_hbm, wo_hbm,
    ctx_hbm, pool_hbm, dec_hbm,
    xs, hd, kc, vc, wq, wkv, wo,
    kvacc, qacc, cosf, sinf, dcos, dsin,
    G, Qs, M, L, ACC, dk, dv, dq,
    tab, gains, PI, NUM, pool, ctxs,
    PS, RS, DO,
    in_sem, out_sem, send_sem, recv_sem,
    rs_send, rs_recv, ag_send, ag_recv,
):
    g = lax.axis_index("group")
    s = lax.axis_index("seq")
    t = lax.axis_index("tp")
    X = g * 2 + rem(s, 2)
    Y = div(s, 2)
    me = g * 8 + s

    place = {}
    for dx, dy in ORDER:
        xx = rem(X + dx, 4)
        yy = rem(Y + dy, 4)
        place[dx, dy] = div(xx, 2), yy * 2 + rem(xx, 2)
    place_shard = {o: gg * 8 + ss for o, (gg, ss) in place.items()}
    num = [g * 0 + i for i in range(64)]
    tps = [rem(t + i, 8) for i in range(8)]
    tp_cols = [pl.ds(pl.multiple_of(u * PIECE, HD), PIECE) for u in tps]

    def at(dx, dy):
        return place[dx, dy]

    def shard(dx, dy):
        return place_shard[dx, dy]

    def load(src, dst, n, now=True):
        c = pltpu.make_async_copy(src, dst, in_sem.at[n])
        if now:
            c.start()
        return c

    n = 0
    first = []
    for i in range(NKC):
        ks = pl.ds(i * KCH, KCH)
        first.append((
            load(x_hbm.at[:, ks], xs.at[pl.ds(0, ROWS), ks], n),
            load(wk_hbm.at[ks, :], wkv.at[ks, pl.ds(0, HD)], n + 1),
            load(wv_hbm.at[ks, :], wkv.at[ks, pl.ds(HD, HD)], n + 2),
        ))
        n += 3
        if i == 0:
            hd_load = load(hd_hbm, hd, n)
            small = (
                load(tab_hbm, tab, n + 1),
                load(qg_hbm, gains.at[0], n + 2),
                load(kg_hbm, gains.at[1], n + 3),
            )
            n += 4
    wq_load = []
    for i in range(NKC):
        ks = pl.ds(i * KCH, KCH)
        wq_load.append(load(wq_hbm.at[ks, :], wq.at[ks, :], n, False))
        n += 1
    kc_load = load(kc_hbm, kc, n, False)
    vc_load = load(vc_hbm, vc, n + 1, False)
    wo_load = load(wo_hbm, wo, n + 2, False)

    bar = pltpu.get_barrier_semaphore()
    for o in ((1, 0), (3, 0), (0, 1), (0, 3)):
        gg, ss = at(*o)
        pl.semaphore_signal(bar, inc=1, device_id=(gg, ss, t), device_id_type=MESH)
    for i in range(1, 8):
        pl.semaphore_signal(bar, inc=1, device_id=(g, s, tps[i]), device_id_type=MESH)

    lane = iota((16, HD), 1)
    want_o = div(lane, 2)
    want_r = rem(lane, 2)
    table = jnp.full((16, HD), -1, I32)
    seen = jnp.zeros((16, HD), I32)
    for v in range(NS):
        hit = want_o == owner_ref[v % 2, v // 2]
        table = jnp.where(hit & (seen == want_r), v, table)
        seen = seen + hit.astype(I32)
    for p in range(NP):
        G[me, p, pl.ds(2 * TOK, 16), :] = table.astype(F32).astype(BF16)

    for c in small:
        c.wait()
    freq = tab[pl.ds(2 * TOK, 1), :]
    sign = jnp.where(iota((1, HD), 1) < HD // 2, -1.0, 1.0).astype(F32)
    for p in range(NP):
        base = (start_ref[p] + me * TOK).astype(F32) * freq
        ca = jnp.cos(base)
        sa = jnp.sin(base) * sign
        cb = tab[pl.ds(0, TOK), :]
        sb = tab[pl.ds(TOK, TOK), :]
        rows = pl.ds(p * TOK, TOK)
        cosf[rows, :] = cb * ca - sb * sa
        sinf[rows, :] = cb * sa + sb * ca
    row = iota((DT, HD), 0)
    pos = rem(row, ST)
    for r in range(DR):
        pos = pos + jnp.where(div(row, ST) == r, clen_ref[r], 0)
    ang = pos.astype(F32) * freq
    dcos[...] = jnp.cos(ang)
    dsin[...] = jnp.sin(ang) * sign

    hd_load.wait()
    xs[pl.ds(ROWS, DT), :] = hd[...].astype(F32).reshape(DT, D).astype(BF16)

    for i in range(NKC):
        for c in first[i]:
            c.wait()
        if i >= NKC - 2:
            for c in wq_load[:2] if i == NKC - 2 else wq_load[2:]:
                c.start()
        ks = pl.ds(i * KCH, KCH)
        part = mm(xs[:, ks], wkv[ks, :])
        if i == 0:
            kvacc[...] = part
        else:
            kvacc[...] += part
    kg = gains[1]
    for p in range(NP):
        rows = pl.ds(p * TOK, TOK)
        G[me, p, pl.ds(0, TOK), :] = norm_rope(kvacc[rows, :HD], kg, cosf[rows, :], sinf[rows, :])
        G[me, p, pl.ds(TOK, TOK), :] = kvacc[rows, HD:].astype(BF16)
    drows = pl.ds(ROWS, DT)
    dk[...] = norm_rope(kvacc[drows, :HD], kg, dcos[...], dsin[...])
    dv[...] = kvacc[drows, HD:].astype(BF16)

    def query_part(i):
        wq_load[i].wait()
        ks = pl.ds(i * KCH, KCH)
        part = mm(xs[:, ks], wq[ks, :])
        if i == 0:
            qacc[...] = part
        else:
            qacc[...] += part

    pl.semaphore_wait(bar, 4 + 7)

    sends = []

    def part_of(j, p, half):
        if half is None:
            return G.at[j, num[p]]
        return G.at[j, num[p], pl.ds(0, TOK) if half == 0 else pl.ds(TOK, CH - TOK)]

    def rid(k, p, half):
        return (k * 2 + p) * 2 + half

    def send(dx, dy, p, half, to):
        k = STEP[((dx - to[0]) % 4, (dy - to[1]) % 4)]
        j = shard(dx, dy)
        ref = part_of(j, p, half)
        gg, ss = at(*to)
        c = pltpu.make_async_remote_copy(
            src_ref=ref, dst_ref=ref,
            send_sem=send_sem.at[num[len(sends)]],
            recv_sem=recv_sem.at[num[rid(k, p, half or 0)]],
            device_id=(gg, ss, t), device_id_type=MESH,
        )
        sends.append(c)
        c.start()

    def arrive(k, p, half):
        j = shard(*ORDER[k])
        ref = part_of(j, p, half)
        pltpu.make_async_remote_copy(
            src_ref=ref, dst_ref=ref, send_sem=send_sem.at[num[0]],
            recv_sem=recv_sem.at[num[rid(k, p, half or 0)]],
            device_id=(g, s, t), device_id_type=MESH,
        ).wait_recv()

    def flip(o, p):
        return o if p == 0 else (o[1], o[0])

    def comm(k, p):
        a, b = flip(ORDER[k], p)
        o = ORDER[k]
        if a == 2 and b == 0 or b == 2:
            arrive(k, p, 0)
            arrive(k, p, 1)
        else:
            arrive(k, p, None)
        if b == 0 and a in (1, 3):
            send(*o, p, 0 if a == 3 else 1, flip((4 - a, 0), p))
        if b == 0:
            send(*o, p, None, flip((0, 1), p))
            send(*o, p, None, flip((0, 3), p))
        if b in (1, 3):
            send(*o, p, 0 if b == 3 else 1, flip((0, 4 - b), p))

    for p in range(NP):
        for d in (1, 3):
            send(0, 0, p, None, flip((d, 0), p))
    for p in range(NP):
        for d in (1, 3):
            send(0, 0, p, None, flip((0, d), p))

    ro = iota((HD, 4 * TOK), 0)
    co = iota((HD, 4 * TOK), 1)
    same_row = (rem(ro, 2) == rem(div(co, TOK), 2)) & (div(rem(ro, 64), 2) == rem(co, 32))
    PI[...] = jnp.where(same_row, 1.0, 0.0).astype(BF16)
    col = iota((16, 4 * TOK), 1)
    number = rem(div(col, 32), 8) * 2 + div(col, 2 * TOK)
    NUM[...] = number.astype(F32)

    for i in range(NKC):
        query_part(i)
        if i == 1:
            kc_load.start()
            vc_load.start()
        if i == 3:
            wo_load.start()
    qg = gains[0]
    for h in range(NH):
        cols = pl.ds(h * HD, HD)
        for p in range(NP):
            rows = pl.ds(p * TOK, TOK)
            Qs[p, h] = norm_rope(qacc[rows, cols], qg, cosf[rows, :], sinf[rows, :])
        dq[:, cols] = norm_rope(qacc[drows, cols], qg, dcos[...], dsin[...])

    def attend(shards, own, rows):
        bodies = [(p, h, r) for p in range(NP) for h in range(NH) for r in range(0, TOK, rows)]

        def scores(p, h, r):
            at_rows = pl.ds(r, rows)
            tiles = []
            for j in shards:
                sc = nt(Qs[p, h, at_rows, :], G[j, p, pl.ds(0, TOK), :])
                if own:
                    sc = jnp.where(iota((rows, TOK), 1) <= iota((rows, TOK), 0) + r, sc, -1e30)
                tiles += [sc[:, :HD], sc[:, HD:]]
            return tiles

        def soft(p, h, r, tiles):
            at_rows = pl.ds(r, rows)
            top = tiles[0]
            for tile in tiles[1:]:
                top = jnp.maximum(top, tile)
            top = jnp.max(top, axis=1, keepdims=True)
            if own:
                new = jnp.broadcast_to(top, (rows, HD))
            else:
                old = M[p, h, at_rows, :]
                new = jnp.maximum(old, top)
            mb = new * SM
            ws = [jnp.exp2(tile * SM - mb) for tile in tiles]
            total = ws[0]
            for w in ws[1:]:
                total = total + w
            M[p, h, at_rows, :] = new
            alpha = None
            if own:
                L[p, h, at_rows, :] = total
            else:
                alpha = jnp.exp2(old * SM - mb)
                L[p, h, at_rows, :] = L[p, h, at_rows, :] * alpha + total
            ws = [w.astype(BF16) for w in ws]
            return [jnp.concatenate(ws[n : n + 2], axis=1) for n in range(0, len(ws), 2)], alpha

        def mix(p, h, r, ws, alpha):
            at_rows = pl.ds(r, rows)
            o = mm(ws[0], G[shards[0], p, pl.ds(TOK, TOK), :])
            for w, j in zip(ws[1:], shards[1:]):
                o = o + mm(w, G[j, p, pl.ds(TOK, TOK), :])
            ACC[p, h, at_rows, :] = o if own else ACC[p, h, at_rows, :] * alpha + o

        sc = scores(*bodies[0])
        waiting = None
        for n, b in enumerate(bodies):
            after = scores(*bodies[n + 1]) if n + 1 < len(bodies) else None
            if waiting is not None:
                mix(*waiting)
            waiting = (*b, *soft(*b, sc))
            sc = after
        mix(*waiting)

    def blocks(j):
        row = G[j, 0, pl.ds(2 * TOK, 16), :].astype(F32)
        number = NUM[...]
        picks = []
        for r in range(2):
            code = jnp.sum(jnp.where(lane == me * 2 + r, row, 0.0), axis=1, keepdims=True)
            picks.append(jnp.where(code == number, 1.0, 0.0).astype(BF16))
        for r in range(2):
            half = pl.ds(r * 64, 64)
            pick = PI[half, :] * jnp.concatenate([picks[r]] * 4, axis=0)
            out = mm(pick[:, : 2 * TOK], G[j, 0, pl.ds(0, 2 * TOK), :])
            out += mm(pick[:, 2 * TOK :], G[j, 1, pl.ds(0, 2 * TOK), :])
            pool[j, half, :] = out.astype(BF16)

    for k, p in ((1, 0), (2, 0), (3, 1), (4, 1)):
        comm(k, p)

    attend((me,), True, TOK)

    kc_load.wait()
    vc_load.wait()
    er = iota((HD, DT), 0)
    ec = iota((HD, DT), 1)
    same = div(er, 16) == div(ec, ST)
    qd = jnp.zeros((HD, HD), F32)
    for h in range(NH):
        pick = same & (rem(er, ST) == rem(ec, ST)) & (rem(div(er, ST), NH) == h)
        qd = qd + mm(jnp.where(pick, 1.0, 0.0).astype(BF16), dq[:, h * HD:(h + 1) * HD])
    qd = qd.astype(BF16)
    sn = nt(qd, dk[...])
    sn = jnp.where(same & (rem(ec, ST) <= rem(er, ST)), sn, -1e30)
    outs = []
    for r in range(DR):
        span = slice(r * 16, r * 16 + 16)
        sr = nt(qd[span], kc[r])
        sr = jnp.where(iota((16, CACHE), 1) < clen_ref[r], sr, -1e30)
        top = jnp.maximum(
            jnp.max(sr, axis=1, keepdims=True), jnp.max(sn[span], axis=1, keepdims=True)
        )
        wr = jnp.exp2((sr - top) * SM)
        wn = jnp.exp2((sn[span] - top) * SM)
        total = jnp.sum(wr, axis=1, keepdims=True) + jnp.sum(wn, axis=1, keepdims=True)
        mixed = mm(wr.astype(BF16), vc[r]) + mm(wn.astype(BF16), dv[...])
        outs.append(mixed / total)
    cd = jnp.concatenate(outs, axis=0).astype(BF16)
    for k, p in ((3, 0), (4, 0), (1, 1), (2, 1)):
        comm(k, p)
    tr = iota((DT, HD), 0)
    tc = iota((DT, HD), 1)
    heads = []
    for h in range(NH):
        pick = (div(tc, 16) == div(tr, ST)) & (rem(tc, ST) == rem(tr, ST)) & (rem(div(tc, ST), NH) == h)
        heads.append(mm(jnp.where(pick, 1.0, 0.0).astype(BF16), cd).astype(BF16))
    dctx = jnp.concatenate(heads, axis=1)
    wo_load.wait()
    for i in range(8):
        PS[i] = mm(dctx, wo[:, i * PIECE:(i + 1) * PIECE]).astype(BF16)
    rsends = []
    for i in range(1, 8):
        to = tps[i]
        c = pltpu.make_async_remote_copy(
            src_ref=PS.at[to], dst_ref=RS.at[t],
            send_sem=rs_send.at[num[i]], recv_sem=rs_recv.at[num[8 - i]],
            device_id=(g, s, to), device_id_type=MESH,
        )
        c.start()
        rsends.append(c)

    for k, p in ((5, 0), (6, 1)):
        comm(k, p)

    asends = []
    mine = tp_cols[0]

    def reduce():
        total = PS[t].astype(F32)
        for i in range(1, 8):
            frm = tps[i]
            pltpu.make_async_remote_copy(
                src_ref=PS.at[frm], dst_ref=RS.at[frm], send_sem=rs_send.at[num[0]],
                recv_sem=rs_recv.at[num[i]], device_id=(g, s, t), device_id_type=MESH,
            ).wait_recv()
            total = total + RS[frm].astype(F32)
        DO[:, :, mine] = total.reshape(DR, ST, PIECE).astype(BF16)
        for i in range(1, 8):
            c = pltpu.make_async_remote_copy(
                src_ref=DO.at[:, :, mine], dst_ref=DO.at[:, :, mine],
                send_sem=ag_send.at[num[i]], recv_sem=ag_recv.at[num[8 - i]],
                device_id=(g, s, tps[i]), device_id_type=MESH,
            )
            c.start()
            asends.append(c)

    @pl.loop(1, NS // 2 + 1)
    def _(turn):
        ja = 0
        jb = 0
        for n in range(1, NS // 2 + 1):
            ja = ja + jnp.where(turn == n, shard(*ORDER[2 * n - 1]), 0)
            jb = jb + jnp.where(turn == n, shard(*ORDER[2 * n]) if 2 * n < NS else NS, 0)

        for when, ks in BLOCKS.items():
            @pl.when(turn == when)
            def _():
                for k in ks:
                    blocks(shard(*ORDER[k]))

        for when, events in LATER.items():
            @pl.when(turn == when)
            def _():
                for k, p in events:
                    comm(k, p)

        @pl.when(turn == 4)
        def _():
            reduce()

        early = jnp.minimum(ja, jb)
        late = jnp.maximum(ja, jb)

        @pl.when(late < me)
        def _():
            attend((early, late), False, TOK)

        @pl.when((early < me) & (late >= me))
        def _():
            attend((early,), False, TOK)

    blocks(shard(*ORDER[15]))
    pool_out = pltpu.make_async_copy(pool, pool_hbm, out_sem.at[0])
    pool_out.start()
    for i in range(1, 8):
        cols = tp_cols[i]
        pltpu.make_async_remote_copy(
            src_ref=DO.at[:, :, cols], dst_ref=DO.at[:, :, cols], send_sem=ag_send.at[num[0]],
            recv_sem=ag_recv.at[num[i]], device_id=(g, s, t), device_id_type=MESH,
        ).wait_recv()
    dec_out = pltpu.make_async_copy(DO, dec_hbm, out_sem.at[1])
    dec_out.start()

    for p in range(NP):
        tok = me * TOK + iota((TOK, HD), 0)
        keep = tok < len_ref[p]
        for h in range(NH):
            total = jnp.sum(L[p, h], axis=1, keepdims=True)
            out = jnp.where(keep, ACC[p, h] / total, 0.0)
            ctxs[pl.ds(p * TOK, TOK), pl.ds(h * HD, HD)] = out.astype(BF16)
    ctx_out = pltpu.make_async_copy(ctxs, ctx_hbm, out_sem.at[2])
    ctx_out.start()
    for c in sends + rsends + asends:
        c.wait_send()
    pool_out.wait()
    dec_out.wait()
    ctx_out.wait()


def deliver(ctx_in, pool_in, dec_in, ctx, pool, dec, sem):
    copies = []
    for i, (a, b) in enumerate(((ctx_in, ctx), (pool_in, pool), (dec_in, dec))):
        c = pltpu.make_async_copy(a, b, sem.at[i])
        c.start()
        copies.append(c)
    for c in copies:
        c.wait()


def tables():
    freq = THETA ** (-np.arange(HD // 2, dtype=np.float64) * 2.0 / HD)
    ang = np.arange(TOK, dtype=np.float64)[:, None] * freq[None, :]
    tab = np.zeros((2 * TOK + 8, HD), np.float32)
    tab[:TOK] = np.concatenate([np.cos(ang), np.cos(ang)], axis=1)
    tab[TOK : 2 * TOK] = np.concatenate([-np.sin(ang), np.sin(ang)], axis=1)
    tab[2 * TOK] = np.concatenate([freq, freq])
    return tab


def per_device(
    prompt_tokens, prompt_lengths, prompt_token_start, block_owner, decode_hidden,
    cache_lengths, key_cache, value_cache, w_query, w_key, w_value, w_out,
    query_gain, key_gain,
):
    sm = pl.BlockSpec(memory_space=pltpu.SMEM)
    hbm = pl.BlockSpec(memory_space=pl.ANY)
    V = pltpu.VMEM
    ctx, pool, dec = pl.pallas_call(
        kernel,
        out_shape=(
            jax.ShapeDtypeStruct((ROWS, NH * HD), BF16),
            jax.ShapeDtypeStruct((NS, HD, HD), BF16),
            jax.ShapeDtypeStruct((DR, ST, D), BF16),
        ),
        in_specs=[sm] * 4 + [hbm] * 11,
        out_specs=(hbm, hbm, hbm),
        scratch_shapes=[
            V((ROWS + DT, D), BF16),
            V((DR, ST, D), BF16),
            V((DR, CACHE, HD), BF16),
            V((DR, CACHE, HD), BF16),
            V((D, NH * HD), BF16),
            V((D, 2 * HD), BF16),
            V((NH * HD, D), BF16),
            V((ROWS + DT, 2 * HD), F32),
            V((ROWS + DT, NH * HD), F32),
            V((ROWS, HD), F32),
            V((ROWS, HD), F32),
            V((DT, HD), F32),
            V((DT, HD), F32),
            V((NS, NP, CH, HD), BF16),
            V((NP, NH, TOK, HD), BF16),
            V((NP, NH, TOK, HD), F32),
            V((NP, NH, TOK, HD), F32),
            V((NP, NH, TOK, HD), F32),
            V((DT, HD), BF16),
            V((DT, HD), BF16),
            V((DT, NH * HD), BF16),
            V((2 * TOK + 8, HD), F32),
            V((2, 1, HD), F32),
            V((HD, 4 * TOK), BF16),
            V((16, 4 * TOK), F32),
            V((NS, HD, HD), BF16),
            V((ROWS, NH * HD), BF16),
            V((8, DT, PIECE), BF16),
            V((8, DT, PIECE), BF16),
            V((DR, ST, D), BF16),
            pltpu.SemaphoreType.DMA((32,)),
            pltpu.SemaphoreType.DMA((3,)),
            pltpu.SemaphoreType.DMA((64,)),
            pltpu.SemaphoreType.DMA((64,)),
            pltpu.SemaphoreType.DMA((8,)),
            pltpu.SemaphoreType.DMA((8,)),
            pltpu.SemaphoreType.DMA((8,)),
            pltpu.SemaphoreType.DMA((8,)),
        ],
        compiler_params=pltpu.CompilerParams(
            collective_id=0, has_side_effects=True, vmem_limit_bytes=58 * 1024 * 1024
        ),
        name="split_attention",
    )(
        prompt_token_start, prompt_lengths,
        block_owner.transpose(1, 2, 0).reshape(NP, 8), cache_lengths,
        jnp.asarray(tables()),
        query_gain.reshape(1, HD), key_gain.reshape(1, HD),
        prompt_tokens.reshape(ROWS, D), decode_hidden, key_cache, value_cache,
        w_query, w_key, w_value, w_out,
    )
    ctx, pool, dec = pl.pallas_call(
        deliver,
        out_shape=(
            jax.ShapeDtypeStruct((ROWS, NH * HD), BF16),
            jax.ShapeDtypeStruct((NS, HD, HD), BF16),
            jax.ShapeDtypeStruct((DR, ST, D), BF16),
        ),
        in_specs=[pl.BlockSpec(memory_space=pltpu.VMEM)] * 3,
        out_specs=(hbm, hbm, hbm),
        scratch_shapes=[pltpu.SemaphoreType.DMA((3,))],
        name="deliver",
    )(ctx, pool, dec)
    return (
        ctx.reshape(NP, TOK, NH * HD),
        pool.reshape(1, 2 * NS, 32, 2, HD),
        dec,
    )


def solution(mesh):
    placed = (
        P(None, ("group", "seq"), None),
        P(),
        P(),
        P(("group", "seq"), None, None),
        P(("group", "seq"), None, None),
        P(("group", "seq")),
        P(("group", "seq"), None, "tp"),
        P(("group", "seq"), None, "tp"),
        P(None, "tp"),
        P(None, "tp"),
        P(None, "tp"),
        P("tp", None),
        P(),
        P(),
    )
    return jax.shard_map(
        per_device,
        mesh=mesh,
        in_specs=placed,
        out_specs=(
            P(None, ("group", "seq"), "tp"),
            P(("group", "seq"), None, None, None, "tp"),
            P(("group", "seq"), None, None),
        ),
        check_vma=False,
    )
```

```python
import numpy as np
import jax
import jax.numpy as jnp
from jax import lax
from jax.experimental import pallas as pl
from jax.experimental.pallas import tpu as pltpu
from jax.sharding import PartitionSpec as P

MESH = pl.DeviceIdType.MESH
F32 = jnp.float32
BF16 = jnp.bfloat16
I32 = jnp.int32

EPS = 1e-06
THETA = 1000000.0
HD = 128
TOK = 256
NP = 2
ROWS = NP * TOK
NH = 4
DR = 8
ST = 4
DT = DR * ST
D = 5120
CACHE = 1024
NS = 16
CH = 2 * TOK + 16
KCH = 1024
NKC = D // KCH
PIECE = D // 8
SM = HD**-0.5 * 1.4426950408889634

ORDER = [
    (0, 0),
    (3, 0), (1, 0), (0, 3), (0, 1),
    (2, 0), (0, 2),
    (3, 3), (1, 1), (3, 1), (1, 3),
    (3, 2), (1, 2), (2, 3), (2, 1),
    (2, 2),
]
STEP = {o: k for k, o in enumerate(ORDER)}
LATER = {
    2: ((7, 0), (8, 0), (7, 1), (8, 1)),
    3: ((9, 0), (10, 0), (9, 1), (10, 1), (5, 1), (6, 0)),
    5: ((13, 0), (14, 0), (11, 1), (12, 1)),
    6: ((11, 0), (12, 0)),
    7: ((13, 1), (14, 1)),
    8: ((15, 0), (15, 1)),
}
BLOCKS = {3: range(0, 4), 5: range(4, 8), 6: range(8, 11), 8: range(11, 15)}


def rem(a, b):
    return lax.rem(a, b) if a.ndim == 0 else a & (b - 1)


def div(a, b):
    return lax.div(a, b) if a.ndim == 0 else lax.shift_right_logical(a, jnp.full(a.shape, b.bit_length() - 1, a.dtype))


def nt(a, b):
    return lax.dot_general(a, b, (((1,), (1,)), ((), ())), preferred_element_type=F32)


def mm(a, b):
    return jnp.dot(a, b, preferred_element_type=F32)


def iota(shape, dim):
    return lax.broadcasted_iota(I32, shape, dim)


def norm_rope(raw, gain, cosine, sine):
    mean_sq = mm((raw * raw).astype(BF16), jnp.full((HD, HD), 1.0 / HD, BF16))
    u = raw * lax.rsqrt(mean_sq + EPS) * gain
    return (u * cosine + pltpu.roll(u, HD // 2, 1) * sine).astype(BF16)


def kernel(
    start_ref, len_ref, owner_ref, clen_ref,
    tab_hbm, qg_hbm, kg_hbm,
    x_hbm, hd_hbm, kc_hbm, vc_hbm, wq_hbm, wk_hbm, wv_hbm, wo_hbm,
    ctx_hbm, pool_hbm, dec_hbm,
    xs, hd, kc, vc, wq, wkv, wo,
    kvacc, qacc, cosf, sinf, dcos, dsin,
    G, Qs, M, L, ACC, dk, dv, dq,
    tab, gains, PI, NUM, pool, ctxs,
    PS, RS, DO,
    in_sem, out_sem, send_sem, recv_sem,
    rs_send, rs_recv, ag_send, ag_recv,
):
    g = lax.axis_index("group")
    s = lax.axis_index("seq")
    t = lax.axis_index("tp")
    X = g * 2 + rem(s, 2)
    Y = div(s, 2)
    me = g * 8 + s

    place = {}
    for dx, dy in ORDER:
        xx = rem(X + dx, 4)
        yy = rem(Y + dy, 4)
        place[dx, dy] = div(xx, 2), yy * 2 + rem(xx, 2)
    place_shard = {o: gg * 8 + ss for o, (gg, ss) in place.items()}
    num = [g * 0 + i for i in range(64)]
    tps = [rem(t + i, 8) for i in range(8)]
    tp_cols = [pl.ds(pl.multiple_of(u * PIECE, HD), PIECE) for u in tps]

    def at(dx, dy):
        return place[dx, dy]

    def shard(dx, dy):
        return place_shard[dx, dy]

    def load(src, dst, n, now=True):
        c = pltpu.make_async_copy(src, dst, in_sem.at[n])
        if now:
            c.start()
        return c

    n = 0
    first = []
    for i in range(NKC):
        ks = pl.ds(i * KCH, KCH)
        first.append((
            load(x_hbm.at[:, ks], xs.at[pl.ds(0, ROWS), ks], n),
            load(wk_hbm.at[ks, :], wkv.at[ks, pl.ds(0, HD)], n + 1),
            load(wv_hbm.at[ks, :], wkv.at[ks, pl.ds(HD, HD)], n + 2),
        ))
        n += 3
        if i == 0:
            hd_load = load(hd_hbm, hd, n)
            small = (
                load(tab_hbm, tab, n + 1),
                load(qg_hbm, gains.at[0], n + 2),
                load(kg_hbm, gains.at[1], n + 3),
            )
            n += 4
    wq_load = []
    for i in range(NKC):
        ks = pl.ds(i * KCH, KCH)
        wq_load.append(load(wq_hbm.at[ks, :], wq.at[ks, :], n, False))
        n += 1
    kc_load = load(kc_hbm, kc, n, False)
    vc_load = load(vc_hbm, vc, n + 1, False)
    wo_load = load(wo_hbm, wo, n + 2, False)

    bar = pltpu.get_barrier_semaphore()
    for o in ((1, 0), (3, 0), (0, 1), (0, 3)):
        gg, ss = at(*o)
        pl.semaphore_signal(bar, inc=1, device_id=(gg, ss, t), device_id_type=MESH)
    for i in range(1, 8):
        pl.semaphore_signal(bar, inc=1, device_id=(g, s, tps[i]), device_id_type=MESH)

    lane = iota((16, HD), 1)
    want_o = div(lane, 2)
    want_r = rem(lane, 2)
    table = jnp.full((16, HD), -1, I32)
    seen = jnp.zeros((16, HD), I32)
    for v in range(NS):
        hit = want_o == owner_ref[v % 2, v // 2]
        table = jnp.where(hit & (seen == want_r), v, table)
        seen = seen + hit.astype(I32)
    for p in range(NP):
        G[me, p, pl.ds(2 * TOK, 16), :] = table.astype(F32).astype(BF16)

    for c in small:
        c.wait()
    freq = tab[pl.ds(2 * TOK, 1), :]
    sign = jnp.where(iota((1, HD), 1) < HD // 2, -1.0, 1.0).astype(F32)
    for p in range(NP):
        base = (start_ref[p] + me * TOK).astype(F32) * freq
        ca = jnp.cos(base)
        sa = jnp.sin(base) * sign
        cb = tab[pl.ds(0, TOK), :]
        sb = tab[pl.ds(TOK, TOK), :]
        rows = pl.ds(p * TOK, TOK)
        cosf[rows, :] = cb * ca - sb * sa
        sinf[rows, :] = cb * sa + sb * ca
    row = iota((DT, HD), 0)
    pos = rem(row, ST)
    for r in range(DR):
        pos = pos + jnp.where(div(row, ST) == r, clen_ref[r], 0)
    ang = pos.astype(F32) * freq
    dcos[...] = jnp.cos(ang)
    dsin[...] = jnp.sin(ang) * sign

    hd_load.wait()
    xs[pl.ds(ROWS, DT), :] = hd[...].astype(F32).reshape(DT, D).astype(BF16)

    for i in range(NKC):
        for c in first[i]:
            c.wait()
        if i >= NKC - 2:
            for c in wq_load[:2] if i == NKC - 2 else wq_load[2:]:
                c.start()
        ks = pl.ds(i * KCH, KCH)
        part = mm(xs[:, ks], wkv[ks, :])
        if i == 0:
            kvacc[...] = part
        else:
            kvacc[...] += part
    kg = gains[1]
    for p in range(NP):
        rows = pl.ds(p * TOK, TOK)
        G[me, p, pl.ds(0, TOK), :] = norm_rope(kvacc[rows, :HD], kg, cosf[rows, :], sinf[rows, :])
        G[me, p, pl.ds(TOK, TOK), :] = kvacc[rows, HD:].astype(BF16)
    drows = pl.ds(ROWS, DT)
    dk[...] = norm_rope(kvacc[drows, :HD], kg, dcos[...], dsin[...])
    dv[...] = kvacc[drows, HD:].astype(BF16)

    def query_part(i):
        wq_load[i].wait()
        ks = pl.ds(i * KCH, KCH)
        part = mm(xs[:, ks], wq[ks, :])
        if i == 0:
            qacc[...] = part
        else:
            qacc[...] += part

    pl.semaphore_wait(bar, 4 + 7)

    sends = []

    def part_of(j, p, half):
        if half is None:
            return G.at[j, num[p]]
        return G.at[j, num[p], pl.ds(0, TOK) if half == 0 else pl.ds(TOK, CH - TOK)]

    def rid(k, p, half):
        return (k * 2 + p) * 2 + half

    def send(dx, dy, p, half, to):
        k = STEP[((dx - to[0]) % 4, (dy - to[1]) % 4)]
        j = shard(dx, dy)
        ref = part_of(j, p, half)
        gg, ss = at(*to)
        c = pltpu.make_async_remote_copy(
            src_ref=ref, dst_ref=ref,
            send_sem=send_sem.at[num[len(sends)]],
            recv_sem=recv_sem.at[num[rid(k, p, half or 0)]],
            device_id=(gg, ss, t), device_id_type=MESH,
        )
        sends.append(c)
        c.start()

    def arrive(k, p, half):
        j = shard(*ORDER[k])
        ref = part_of(j, p, half)
        pltpu.make_async_remote_copy(
            src_ref=ref, dst_ref=ref, send_sem=send_sem.at[num[0]],
            recv_sem=recv_sem.at[num[rid(k, p, half or 0)]],
            device_id=(g, s, t), device_id_type=MESH,
        ).wait_recv()

    def flip(o, p):
        return o if p == 0 else (o[1], o[0])

    def comm(k, p):
        a, b = flip(ORDER[k], p)
        o = ORDER[k]
        if a == 2 and b == 0 or b == 2:
            arrive(k, p, 0)
            arrive(k, p, 1)
        else:
            arrive(k, p, None)
        if b == 0 and a in (1, 3):
            send(*o, p, 0 if a == 3 else 1, flip((4 - a, 0), p))
        if b == 0:
            send(*o, p, None, flip((0, 1), p))
            send(*o, p, None, flip((0, 3), p))
        if b in (1, 3):
            send(*o, p, 0 if b == 3 else 1, flip((0, 4 - b), p))

    for p in range(NP):
        for d in (1, 3):
            send(0, 0, p, None, flip((d, 0), p))
    for p in range(NP):
        for d in (1, 3):
            send(0, 0, p, None, flip((0, d), p))

    ro = iota((HD, 4 * TOK), 0)
    co = iota((HD, 4 * TOK), 1)
    same_row = (rem(ro, 2) == rem(div(co, TOK), 2)) & (div(rem(ro, 64), 2) == rem(co, 32))
    PI[...] = jnp.where(same_row, 1.0, 0.0).astype(BF16)
    col = iota((16, 4 * TOK), 1)
    number = rem(div(col, 32), 8) * 2 + div(col, 2 * TOK)
    NUM[...] = number.astype(F32)

    for i in range(NKC):
        query_part(i)
        if i == 1:
            kc_load.start()
            vc_load.start()
        if i == 3:
            wo_load.start()
    qg = gains[0]
    for h in range(NH):
        cols = pl.ds(h * HD, HD)
        for p in range(NP):
            rows = pl.ds(p * TOK, TOK)
            Qs[p, h] = norm_rope(qacc[rows, cols], qg, cosf[rows, :], sinf[rows, :])
        dq[:, cols] = norm_rope(qacc[drows, cols], qg, dcos[...], dsin[...])

    def attend(shards, own, rows):
        bodies = [(p, h, r) for p in range(NP) for h in range(NH) for r in range(0, TOK, rows)]

        def scores(p, h, r):
            at_rows = pl.ds(r, rows)
            tiles = []
            for j in shards:
                sc = nt(Qs[p, h, at_rows, :], G[j, p, pl.ds(0, TOK), :])
                if own:
                    sc = jnp.where(iota((rows, TOK), 1) <= iota((rows, TOK), 0) + r, sc, -1e30)
                tiles += [sc[:, :HD], sc[:, HD:]]
            return tiles

        def soft(p, h, r, tiles):
            at_rows = pl.ds(r, rows)
            top = tiles[0]
            for tile in tiles[1:]:
                top = jnp.maximum(top, tile)
            top = jnp.max(top, axis=1, keepdims=True) * SM
            if own:
                new = jnp.broadcast_to(top, (rows, HD))
            else:
                old = M[p, h, at_rows, :]
                new = jnp.maximum(old, top)
            ws = [jnp.exp2(tile * SM - new) for tile in tiles]
            total = ws[0]
            for w in ws[1:]:
                total = total + w
            M[p, h, at_rows, :] = new
            alpha = None
            if own:
                L[p, h, at_rows, :] = total
            else:
                alpha = jnp.exp2(old - new)
                L[p, h, at_rows, :] = L[p, h, at_rows, :] * alpha + total
            ws = [w.astype(BF16) for w in ws]
            return [jnp.concatenate(ws[n : n + 2], axis=1) for n in range(0, len(ws), 2)], alpha

        def mix(p, h, r, ws, alpha):
            at_rows = pl.ds(r, rows)
            o = mm(ws[0], G[shards[0], p, pl.ds(TOK, TOK), :])
            for w, j in zip(ws[1:], shards[1:]):
                o = o + mm(w, G[j, p, pl.ds(TOK, TOK), :])
            ACC[p, h, at_rows, :] = o if own else ACC[p, h, at_rows, :] * alpha + o

        sc = scores(*bodies[0])
        waiting = None
        for n, b in enumerate(bodies):
            after = scores(*bodies[n + 1]) if n + 1 < len(bodies) else None
            if waiting is not None:
                mix(*waiting)
            waiting = (*b, *soft(*b, sc))
            sc = after
        mix(*waiting)

    def blocks(j):
        row = G[j, 0, pl.ds(2 * TOK, 16), :].astype(F32)
        number = NUM[...]
        picks = []
        for r in range(2):
            code = jnp.sum(jnp.where(lane == me * 2 + r, row, 0.0), axis=1, keepdims=True)
            picks.append(jnp.where(code == number, 1.0, 0.0).astype(BF16))
        for r in range(2):
            half = pl.ds(r * 64, 64)
            pick = PI[half, :] * jnp.concatenate([picks[r]] * 4, axis=0)
            out = mm(pick[:, : 2 * TOK], G[j, 0, pl.ds(0, 2 * TOK), :])
            out += mm(pick[:, 2 * TOK :], G[j, 1, pl.ds(0, 2 * TOK), :])
            pool[j, half, :] = out.astype(BF16)

    for k, p in ((1, 0), (2, 0), (3, 1), (4, 1)):
        comm(k, p)

    attend((me,), True, TOK)

    kc_load.wait()
    vc_load.wait()
    er = iota((HD, DT), 0)
    ec = iota((HD, DT), 1)
    same = div(er, 16) == div(ec, ST)
    qd = jnp.zeros((HD, HD), F32)
    for h in range(NH):
        pick = same & (rem(er, ST) == rem(ec, ST)) & (rem(div(er, ST), NH) == h)
        qd = qd + mm(jnp.where(pick, 1.0, 0.0).astype(BF16), dq[:, h * HD:(h + 1) * HD])
    qd = qd.astype(BF16)
    sn = nt(qd, dk[...])
    sn = jnp.where(same & (rem(ec, ST) <= rem(er, ST)), sn, -1e30)
    outs = []
    ahead = [nt(qd[:16], kc[0]), nt(qd[16:32], kc[1])]
    for r in range(DR):
        span = slice(r * 16, r * 16 + 16)
        if r + 2 < DR:
            ahead.append(nt(qd[r * 16 + 32 : r * 16 + 48], kc[r + 2]))
        sr = ahead[r]
        sr = jnp.where(iota((16, CACHE), 1) < clen_ref[r], sr, -1e30)
        top = jnp.maximum(
            jnp.max(sr, axis=1, keepdims=True), jnp.max(sn[span], axis=1, keepdims=True)
        )
        wr = jnp.exp2((sr - top) * SM)
        wn = jnp.exp2((sn[span] - top) * SM)
        total = jnp.sum(wr, axis=1, keepdims=True) + jnp.sum(wn, axis=1, keepdims=True)
        mixed = mm(wr.astype(BF16), vc[r]) + mm(wn.astype(BF16), dv[...])
        outs.append(mixed / total)
    cd = jnp.concatenate(outs, axis=0).astype(BF16)
    for k, p in ((3, 0), (4, 0), (1, 1), (2, 1)):
        comm(k, p)
    tr = iota((DT, HD), 0)
    tc = iota((DT, HD), 1)
    heads = []
    for h in range(NH):
        pick = (div(tc, 16) == div(tr, ST)) & (rem(tc, ST) == rem(tr, ST)) & (rem(div(tc, ST), NH) == h)
        heads.append(mm(jnp.where(pick, 1.0, 0.0).astype(BF16), cd).astype(BF16))
    dctx = jnp.concatenate(heads, axis=1)
    wo_load.wait()
    for i in range(8):
        PS[i] = mm(dctx, wo[:, i * PIECE:(i + 1) * PIECE]).astype(BF16)
    rsends = []
    for i in range(1, 8):
        to = tps[i]
        c = pltpu.make_async_remote_copy(
            src_ref=PS.at[to], dst_ref=RS.at[t],
            send_sem=rs_send.at[num[i]], recv_sem=rs_recv.at[num[8 - i]],
            device_id=(g, s, to), device_id_type=MESH,
        )
        c.start()
        rsends.append(c)

    for k, p in ((5, 0), (6, 1)):
        comm(k, p)

    asends = []
    mine = tp_cols[0]

    def reduce():
        total = PS[t].astype(F32)
        for i in range(1, 8):
            frm = tps[i]
            pltpu.make_async_remote_copy(
                src_ref=PS.at[frm], dst_ref=RS.at[frm], send_sem=rs_send.at[num[0]],
                recv_sem=rs_recv.at[num[i]], device_id=(g, s, t), device_id_type=MESH,
            ).wait_recv()
            total = total + RS[frm].astype(F32)
        DO[:, :, mine] = total.reshape(DR, ST, PIECE).astype(BF16)
        for i in range(1, 8):
            c = pltpu.make_async_remote_copy(
                src_ref=DO.at[:, :, mine], dst_ref=DO.at[:, :, mine],
                send_sem=ag_send.at[num[i]], recv_sem=ag_recv.at[num[8 - i]],
                device_id=(g, s, tps[i]), device_id_type=MESH,
            )
            c.start()
            asends.append(c)

    @pl.loop(1, NS // 2 + 1)
    def _(turn):
        ja = 0
        jb = 0
        for n in range(1, NS // 2 + 1):
            ja = ja + jnp.where(turn == n, shard(*ORDER[2 * n - 1]), 0)
            jb = jb + jnp.where(turn == n, shard(*ORDER[2 * n]) if 2 * n < NS else NS, 0)

        for when, ks in BLOCKS.items():
            @pl.when(turn == when)
            def _():
                for k in ks:
                    blocks(shard(*ORDER[k]))

        for when, events in LATER.items():
            @pl.when(turn == when)
            def _():
                for k, p in events:
                    comm(k, p)

        @pl.when(turn == 5)
        def _():
            reduce()

        early = jnp.minimum(ja, jb)
        late = jnp.maximum(ja, jb)

        @pl.when(late < me)
        def _():
            attend((early, late), False, TOK)

        @pl.when((early < me) & (late >= me))
        def _():
            attend((early,), False, TOK)

    blocks(shard(*ORDER[15]))
    pool_out = pltpu.make_async_copy(pool, pool_hbm, out_sem.at[0])
    pool_out.start()
    for i in range(1, 8):
        cols = tp_cols[i]
        pltpu.make_async_remote_copy(
            src_ref=DO.at[:, :, cols], dst_ref=DO.at[:, :, cols], send_sem=ag_send.at[num[0]],
            recv_sem=ag_recv.at[num[i]], device_id=(g, s, t), device_id_type=MESH,
        ).wait_recv()
    dec_out = pltpu.make_async_copy(DO, dec_hbm, out_sem.at[1])
    dec_out.start()

    ctx_outs = []
    for p in range(NP):
        tok = me * TOK + iota((TOK, HD), 0)
        keep = tok < len_ref[p]
        for h in range(NH):
            total = jnp.sum(L[p, h], axis=1, keepdims=True)
            out = jnp.where(keep, ACC[p, h] / total, 0.0)
            ctxs[pl.ds(p * TOK, TOK), pl.ds(h * HD, HD)] = out.astype(BF16)
        rows = pl.ds(p * TOK, TOK)
        ctx_outs.append(pltpu.make_async_copy(ctxs.at[rows], ctx_hbm.at[rows], out_sem.at[2 + p]))
        ctx_outs[p].start()
    for c in sends + rsends + asends:
        c.wait_send()
    pool_out.wait()
    dec_out.wait()
    for c in ctx_outs:
        c.wait()


def deliver(ctx_in, pool_in, dec_in, ctx, pool, dec, ctx_v, pool_v, dec_v, rsem, wsem):
    reads = []
    writes = []
    for i, (a, v, b) in enumerate(((ctx_in, ctx_v, ctx), (pool_in, pool_v, pool), (dec_in, dec_v, dec))):
        half = a.shape[0] // 2
        for n in range(2):
            part = pl.ds(n * half, half)
            reads.append(pltpu.make_async_copy(a.at[part], v.at[part], rsem.at[2 * i + n]))
            writes.append(pltpu.make_async_copy(v.at[part], b.at[part], wsem.at[2 * i + n]))
    for c in reads:
        c.start()
    for c, w in zip(reads, writes):
        c.wait()
        w.start()
    for w in writes:
        w.wait()


def tables():
    freq = THETA ** (-np.arange(HD // 2, dtype=np.float64) * 2.0 / HD)
    ang = np.arange(TOK, dtype=np.float64)[:, None] * freq[None, :]
    tab = np.zeros((2 * TOK + 8, HD), np.float32)
    tab[:TOK] = np.concatenate([np.cos(ang), np.cos(ang)], axis=1)
    tab[TOK : 2 * TOK] = np.concatenate([-np.sin(ang), np.sin(ang)], axis=1)
    tab[2 * TOK] = np.concatenate([freq, freq])
    return tab


def per_device(
    prompt_tokens, prompt_lengths, prompt_token_start, block_owner, decode_hidden,
    cache_lengths, key_cache, value_cache, w_query, w_key, w_value, w_out,
    query_gain, key_gain,
):
    sm = pl.BlockSpec(memory_space=pltpu.SMEM)
    hbm = pl.BlockSpec(memory_space=pl.ANY)
    V = pltpu.VMEM
    ctx, pool, dec = pl.pallas_call(
        kernel,
        out_shape=(
            jax.ShapeDtypeStruct((ROWS, NH * HD), BF16),
            jax.ShapeDtypeStruct((NS, HD, HD), BF16),
            jax.ShapeDtypeStruct((DR, ST, D), BF16),
        ),
        in_specs=[sm] * 4 + [hbm] * 11,
        out_specs=(hbm, hbm, hbm),
        scratch_shapes=[
            V((ROWS + DT, D), BF16),
            V((DR, ST, D), BF16),
            V((DR, CACHE, HD), BF16),
            V((DR, CACHE, HD), BF16),
            V((D, NH * HD), BF16),
            V((D, 2 * HD), BF16),
            V((NH * HD, D), BF16),
            V((ROWS + DT, 2 * HD), F32),
            V((ROWS + DT, NH * HD), F32),
            V((ROWS, HD), F32),
            V((ROWS, HD), F32),
            V((DT, HD), F32),
            V((DT, HD), F32),
            V((NS, NP, CH, HD), BF16),
            V((NP, NH, TOK, HD), BF16),
            V((NP, NH, TOK, HD), F32),
            V((NP, NH, TOK, HD), F32),
            V((NP, NH, TOK, HD), F32),
            V((DT, HD), BF16),
            V((DT, HD), BF16),
            V((DT, NH * HD), BF16),
            V((2 * TOK + 8, HD), F32),
            V((2, 1, HD), F32),
            V((HD, 4 * TOK), BF16),
            V((16, 4 * TOK), F32),
            V((NS, HD, HD), BF16),
            V((ROWS, NH * HD), BF16),
            V((8, DT, PIECE), BF16),
            V((8, DT, PIECE), BF16),
            V((DR, ST, D), BF16),
            pltpu.SemaphoreType.DMA((32,)),
            pltpu.SemaphoreType.DMA((4,)),
            pltpu.SemaphoreType.DMA((64,)),
            pltpu.SemaphoreType.DMA((64,)),
            pltpu.SemaphoreType.DMA((8,)),
            pltpu.SemaphoreType.DMA((8,)),
            pltpu.SemaphoreType.DMA((8,)),
            pltpu.SemaphoreType.DMA((8,)),
        ],
        compiler_params=pltpu.CompilerParams(
            collective_id=0, has_side_effects=True, vmem_limit_bytes=58 * 1024 * 1024
        ),
        name="split_attention",
    )(
        prompt_token_start, prompt_lengths,
        block_owner.transpose(1, 2, 0).reshape(NP, 8), cache_lengths,
        jnp.asarray(tables()),
        query_gain.reshape(1, HD), key_gain.reshape(1, HD),
        prompt_tokens.reshape(ROWS, D), decode_hidden, key_cache, value_cache,
        w_query, w_key, w_value, w_out,
    )
    ctx, pool, dec = pl.pallas_call(
        deliver,
        out_shape=(
            jax.ShapeDtypeStruct((ROWS, NH * HD), BF16),
            jax.ShapeDtypeStruct((NS, HD, HD), BF16),
            jax.ShapeDtypeStruct((DR, ST, D), BF16),
        ),
        in_specs=[hbm] * 3,
        out_specs=(hbm, hbm, hbm),
        scratch_shapes=[
            V((ROWS, NH * HD), BF16),
            V((NS, HD, HD), BF16),
            V((DR, ST, D), BF16),
            pltpu.SemaphoreType.DMA((6,)),
            pltpu.SemaphoreType.DMA((6,)),
        ],
        compiler_params=pltpu.CompilerParams(vmem_limit_bytes=58 * 1024 * 1024),
        name="deliver",
    )(ctx, pool, dec)
    return (
        ctx.reshape(NP, TOK, NH * HD),
        pool.reshape(1, 2 * NS, 32, 2, HD),
        dec,
    )


def solution(mesh):
    placed = (
        P(None, ("group", "seq"), None),
        P(),
        P(),
        P(("group", "seq"), None, None),
        P(("group", "seq"), None, None),
        P(("group", "seq")),
        P(("group", "seq"), None, "tp"),
        P(("group", "seq"), None, "tp"),
        P(None, "tp"),
        P(None, "tp"),
        P(None, "tp"),
        P("tp", None),
        P(),
        P(),
    )
    return jax.shard_map(
        per_device,
        mesh=mesh,
        in_specs=placed,
        out_specs=(
            P(None, ("group", "seq"), "tp"),
            P(("group", "seq"), None, None, None, "tp"),
            P(("group", "seq"), None, None),
        ),
        check_vma=False,
    )
```
